32 devices in a mesh: pipe: 4 (over y, x), dp: 8 (over z, core).
Axes of the slice: x: 2, y: 2, z: 4, core: 2. Of those that a mesh axis runs over, the one named last changes fastest.
Arguments:
- queries: bfloat16 [4, 2, 4096, 4096], P('pipe', None, 'dp'), may hold values from -64 to 64
- keys: bfloat16 [4, 2, 4096, 512], P('pipe', None, 'dp'), may hold values from -6 to 6
- values: bfloat16 [4, 2, 4096, 512], P('pipe', None, 'dp'), may hold values from -6 to 6
- segment: int32 [4, 2, 4096], P('pipe', None, 'dp'), may hold values from 0 to 4095, as said below
- parent: int32 [4, 2, 4096], P('pipe', None, 'dp'), may hold values from 0 to 4094, as said below
- tree_lengths: int32 [4, 2, 32], P('pipe'), may hold values from 0 to 3, as said below
Outputs:
- forward_next: bfloat16 [4, 4096, 4096], P('pipe', 'dp')
- return_next: bfloat16 [4, 4096, 4096], P('pipe', 'dp')
The draws below stay inside these ranges and needn't reach their ends.
Inputs may be any that keep to these rules, and one draw needn't show every extreme that they name: `tree_lengths`: each row lists the trees of one micro-batch in order: entries of 1 to 3 blocks that sum to 32, then zeros; some tree is exactly 3 blocks long. Within a micro-batch a segment is a run of rows, numbered by the index of its first row; every tree's first row opens a new segment, so no segment spans two trees; the last row of every micro-batch opens a segment of its own. The first segment of a tree is its own parent; every other segment's parent is an earlier segment of the same tree whose parent is that first segment; in every micro-batch the last row's parent is the segment opened by the row before it.
All inputs are finite; a program needn't handle non-finite values.
Results may differ from the reference program's by a relative error of at most 0.0036.
Values may be sent and summed in bfloat16 or wider, within the bound.
No kernel may reach another device: no remote copies, remote signals or barrier semaphores. Data moves between devices by JAX's collectives and lax.ppermute only.
A program may use at most 192 MiB of HBM per device.

```python
import math
import jax
import jax.numpy as jnp
from jax import lax

BLK = 128
TREE_MOST = 3
KV_HEADS = 4
GROUP = 8
HEAD = 128
PATHS = 2
ROWS = 4096
BLOCKS = 32
N_PIPE = 4


def layout_draw(key):
    block_shape = (N_PIPE, PATHS, BLOCKS)
    row_shape = (N_PIPE, PATHS, ROWS)
    raw = jax.random.randint(jax.random.fold_in(key, 11), block_shape, 1, TREE_MOST + 1, dtype=jnp.int32)
    block_ids = jnp.arange(BLOCKS, dtype=jnp.int32)
    raw = jnp.where(block_ids == 0, TREE_MOST, raw).astype(jnp.int32)
    ends = jnp.cumsum(raw, axis=-1).astype(jnp.int32)
    starts = ends - raw
    lengths = jnp.where(starts < BLOCKS, jnp.minimum(raw, BLOCKS - starts), 0).astype(jnp.int32)
    inside = (starts[..., None, :] <= block_ids[:, None]) & (lengths[..., None, :] > 0)
    tree_first = jnp.max(jnp.where(inside, starts[..., None, :], 0), axis=-1).astype(jnp.int32)
    row_ids = jnp.arange(ROWS, dtype=jnp.int32)
    row_first = (jnp.repeat(tree_first, BLK, axis=-1) * BLK).astype(jnp.int32)
    broken = jax.random.randint(jax.random.fold_in(key, 12), row_shape, 0, 40, dtype=jnp.int32) == 0
    fresh = broken | (row_ids == row_first) | (row_ids >= ROWS - 2)
    opening = lax.cummax(jnp.where(fresh, row_ids, 0).astype(jnp.int32), axis=2)
    segment = opening.astype(jnp.int32)
    root = row_first
    grouping = (jax.random.randint(jax.random.fold_in(key, 13), row_shape, 0, 4, dtype=jnp.int32) == 0) | (row_ids == row_first) | (row_ids == ROWS - 2)
    grouping = grouping & (row_ids != ROWS - 1)
    segment_groups = jnp.take_along_axis(grouping, opening, axis=-1)
    marks = jnp.where(fresh & grouping, segment, -1).astype(jnp.int32)
    latest = lax.cummax(marks, axis=2)
    parent = jnp.where(segment_groups, root, latest).astype(jnp.int32)
    return (lengths, segment, parent)


def score_draw(key):
    key_shape = (N_PIPE, PATHS, ROWS, KV_HEADS, HEAD)
    query_shape = (N_PIPE, PATHS, ROWS, KV_HEADS, GROUP, HEAD)
    key_part = jax.random.fold_in(key, 21)
    query_part = jax.random.fold_in(key, 22)
    keyset = jnp.clip(jax.random.normal(key_part, key_shape, jnp.float32), -6.0, 6.0)
    queryset = jnp.clip(jax.random.normal(query_part, query_shape, jnp.float32), -6.0, 6.0)
    return (queryset.reshape(N_PIPE, PATHS, ROWS, -1), keyset.reshape(N_PIPE, PATHS, ROWS, -1))


def draw_queries(key, part):
    return score_draw(key)[0].astype(jnp.bfloat16)


def draw_keys(key, part):
    return score_draw(key)[1].astype(jnp.bfloat16)


def draw_segment(key, part):
    return layout_draw(key)[1]


def draw_parent(key, part):
    return layout_draw(key)[2]


def draw_tree_lengths(key, part):
    return layout_draw(key)[0]


def block_levels(own_key, dims, cuts, least, largest):
    def one(dim, shards_of):
        heights = jax.random.uniform(jax.random.fold_in(jax.random.fold_in(own_key, 6), dim), (shards_of,), jnp.float32, least / len(cuts), largest / len(cuts))
        return jnp.repeat(jnp.exp(heights), dims[dim] // shards_of).reshape((-1,) + (1,) * (len(dims) - dim - 1))

    gain = one(*cuts[0])
    for cut in cuts[1:]:
        gain = gain * one(*cut)
    return gain


def centred(own_key, shape, deviation, bound, split=(), held_as=jnp.bfloat16):
    values = jax.random.normal(own_key, shape, jnp.float32) * deviation
    if len(split) > 0:
        values = block_levels(own_key, shape, split, -0.22, 0.18) * values
    return jnp.clip(values, min=-bound, max=bound).astype(held_as)


def setup_inputs(seed: int = 0) -> dict:
    streams_of = jax.random.split(jax.random.key(seed), 7)
    queries = draw_queries(jax.random.fold_in(streams_of[6], 71), 0)
    keys = draw_keys(jax.random.fold_in(streams_of[6], 71), 0)
    values = centred(streams_of[2], (N_PIPE, PATHS, ROWS, KV_HEADS * HEAD), 1.0, 6.0, ((0, 4), (2, 8)))
    segment = draw_segment(jax.random.fold_in(streams_of[6], 71), 0)
    parent = draw_parent(jax.random.fold_in(streams_of[6], 71), 0)
    tree_lengths = draw_tree_lengths(jax.random.fold_in(streams_of[6], 71), 0)
    return dict(queries=queries, keys=keys, values=values, segment=segment, parent=parent, tree_lengths=tree_lengths)


NEG = -1e+30

def tree_index(lengths):
    ends = jnp.cumsum(lengths).astype(jnp.int32)
    starts = ends - lengths
    blocks = jnp.arange(lengths.shape[0], dtype=jnp.int32)
    inside = (starts[None, :] <= blocks[:, None]) & (lengths[None, :] > 0)
    return lax.optimization_barrier(jnp.sum(inside.astype(jnp.int32), axis=1)) - 1

def pad_front(array, fill, reach):
    padding = jnp.full((reach,) + array.shape[1:], fill, array.dtype)
    return jnp.concatenate([padding, array], axis=0)

def micro_batch(operands):
    queries, keys, values, segment, parent, lengths = operands
    reach = (TREE_MOST - 1) * BLK
    span = TREE_MOST * BLK
    tree = jnp.repeat(tree_index(lengths), BLK).astype(jnp.int32)
    position = jnp.arange(ROWS, dtype=jnp.int32)
    key_rows = pad_front(keys, 0, reach)
    value_rows = pad_front(values, 0, reach)
    key_tree = pad_front(tree, -2, reach)
    key_pos = pad_front(position, -1, reach)
    key_seg = pad_front(segment, -3, reach)
    key_par = pad_front(parent, -4, reach)
    scale = 1.0 / math.sqrt(HEAD)

    def one_block(index):
        start = (index * BLK).astype(jnp.int32)
        query = lax.dynamic_slice_in_dim(queries, start, BLK, 0).astype(jnp.float32).reshape(BLK, KV_HEADS, GROUP, HEAD)
        keyset = lax.dynamic_slice_in_dim(key_rows, start, span, 0).astype(jnp.float32).reshape(span, KV_HEADS, HEAD)
        valueset = lax.dynamic_slice_in_dim(value_rows, start, span, 0).astype(jnp.float32).reshape(span, KV_HEADS, HEAD)
        query_tree = lax.dynamic_slice_in_dim(tree, start, BLK, 0)
        query_pos = lax.dynamic_slice_in_dim(position, start, BLK, 0)
        query_seg = lax.dynamic_slice_in_dim(segment, start, BLK, 0)
        query_par = lax.dynamic_slice_in_dim(parent, start, BLK, 0)
        window_tree = lax.dynamic_slice_in_dim(key_tree, start, span, 0)
        window_pos = lax.dynamic_slice_in_dim(key_pos, start, span, 0)
        window_seg = lax.dynamic_slice_in_dim(key_seg, start, span, 0)
        window_par = lax.dynamic_slice_in_dim(key_par, start, span, 0)
        related = (window_seg[None, :] == query_seg[:, None]) | (window_seg[None, :] == query_par[:, None]) | (window_par == window_seg)[None, :]
        allowed = (window_tree[None, :] == query_tree[:, None]) & (window_pos[None, :] <= query_pos[:, None]) & related
        scores = jnp.einsum('qhgd,khd->hgqk', query, keyset) * scale
        scores = jnp.where(allowed[None, None], scores, NEG)
        top = lax.optimization_barrier(jnp.max(scores, axis=-1, keepdims=True))
        weights = jnp.exp(scores - top)
        totals = lax.optimization_barrier(jnp.sum(weights, axis=-1))
        rounded = lax.optimization_barrier(weights.astype(jnp.bfloat16)).astype(jnp.float32)
        mixed = jnp.einsum('hgqk,khd->qhgd', rounded, valueset)
        totals = jnp.transpose(totals, (2, 0, 1))[..., None]
        return (mixed / totals).astype(jnp.bfloat16).reshape(BLK, KV_HEADS * GROUP * HEAD)
    result = lax.map(one_block, jnp.arange(BLOCKS, dtype=jnp.int32))
    return result.reshape(ROWS, KV_HEADS * GROUP * HEAD)

def reference(queries, keys, values, segment, parent, tree_lengths):
    count = N_PIPE * PATHS
    operands = (queries.reshape(count, ROWS, -1), keys.reshape(count, ROWS, -1), values.reshape(count, ROWS, -1), segment.reshape(count, ROWS), parent.reshape(count, ROWS), tree_lengths.reshape(count, BLOCKS))
    context = lax.map(micro_batch, operands).reshape(N_PIPE, PATHS, ROWS, -1)
    forward_next = jnp.concatenate([context[0:1, 1], context[:-1, 0]], axis=0)
    return_next = jnp.concatenate([context[1:, 1], context[-1:, 0]], axis=0)
    return (forward_next, return_next)
```

```python
import functools
import math

import jax
import jax.numpy as jnp
from jax import lax
from jax.experimental import pallas as pl
from jax.experimental.pallas import tpu as pltpu
from jax.sharding import PartitionSpec as P

BLK = 128
TREE_MOST = 3
HEAD = 128
REACH = (TREE_MOST - 1) * BLK
SPAN = TREE_MOST * BLK
NEG = -1e30
TOGETHER = 8
FACTOR = math.log2(math.e) / math.sqrt(HEAD)

VMEM_LIMIT = 60 * 1024 * 1024

ANY = pl.BlockSpec(memory_space=pl.ANY)
HBM = pl.BlockSpec(memory_space=pltpu.HBM)
VMEM = pl.BlockSpec(memory_space=pltpu.VMEM)
SMEM = pl.BlockSpec(memory_space=pltpu.SMEM)


def pick(table, index):
    value = jnp.int32(table[-1])
    for at in range(len(table) - 1):
        value = jnp.where(index == at, jnp.int32(table[at]), value)
    return value


def attend_kernel(blocks, halo, pack, *refs):
    refs = list(refs)
    lengths_in, queries, keys, values, seg_in, par_in = refs[:6]
    refs = refs[6:]
    if halo:
        halo_kv, halo_info = refs[:2]
        refs = refs[2:]
    out = refs.pop(0)
    if pack:
        pack_kv, pack_info = refs[:2]
        refs = refs[2:]
    kbuf, vbuf, bias, seg, par, lengths, counter, sems = refs[:8]
    if pack:
        held_kv = refs[8]
    kv_heads = keys.shape[2] // HEAD
    width = queries.shape[2] // kv_heads
    group = width // HEAD
    rows = keys.shape[1]
    lead = REACH if halo else 0
    swap_path = lax.rem(lax.axis_index("pipe"), 2)
    first_block = lax.axis_index("dp") * (rows // BLK)

    copies = []
    packing = []
    count = 0

    def start(source, target, group_of):
        copy = pltpu.make_async_copy(source, target, sems.at[len(copies) + len(packing)])
        copy.start()
        group_of.append(copy)

    start(seg_in, seg, copies)
    start(par_in, par, copies)
    start(lengths_in, lengths, copies)
    for payload in sorted({payload for payload, _ in blocks}):
        path = swap_path if payload == 0 else 1 - swap_path
        for which, (source, target) in enumerate(((keys, kbuf), (values, vbuf))):
            start(source.at[path], target.at[payload, pl.ds(lead, rows)], copies)
            if halo:
                start(halo_kv.at[which, path], target.at[payload, pl.ds(0, lead)], copies)
    if pack:
        for path in range(2):
            for which, source in enumerate((keys, values)):
                start(source.at[path, pl.ds(rows - REACH, REACH)], held_kv.at[which, path], copies)
    for copy in copies:
        copy.wait()
    if pack:
        start(held_kv, pack_kv, packing)
        pack_info[0] = seg[:, rows - REACH :]
        pack_info[1] = par[:, rows - REACH :]

    def build_bias(place, payload, block):
        path = swap_path if payload == 0 else 1 - swap_path
        here = first_block + block

        def step(entry, carry):
            end, begin = carry
            end = end + lengths[path, entry]
            return (end, jnp.where(end <= here, end, begin))

        _, begin = lax.fori_loop(0, lengths.shape[1], step, (jnp.int32(0), jnp.int32(0)))

        def chosen(array, at):
            lanes = slice(at, at + BLK)
            return jnp.where(path == 0, array[0:1, lanes], array[1:2, lanes])

        def column(row):
            return jnp.transpose(jnp.broadcast_to(row, (BLK, BLK)))

        query_seg = column(chosen(seg, block * BLK))
        query_par = column(chosen(par, block * BLK))
        for back in range(TREE_MOST):
            key_block = block - (TREE_MOST - 1) + back
            if key_block >= 0:
                key_seg = chosen(seg, key_block * BLK)
                key_par = chosen(par, key_block * BLK)
            else:
                at = REACH + key_block * BLK
                key_seg = chosen(halo_info.at[0], at)
                key_par = chosen(halo_info.at[1], at)
            related = (key_seg == query_seg) | (key_seg == query_par) | (key_par == key_seg)
            if back == TREE_MOST - 1:
                causal = lax.broadcasted_iota(jnp.int32, (BLK, BLK), 1) <= lax.broadcasted_iota(
                    jnp.int32, (BLK, BLK), 0
                )
                allowed = related & causal
            else:
                allowed = related & (first_block + key_block >= begin)
            bias[place, :, back * BLK : (back + 1) * BLK] = jnp.where(allowed, 0.0, NEG)

    payload_of = functools.partial(pick, [payload for payload, _ in blocks])
    block_of = functools.partial(pick, [block for _, block in blocks])

    def path_of(place):
        payload = payload_of(place)
        return jnp.where(payload == 0, swap_path, 1 - swap_path)

    counter[0] = 0

    def body(query_ref, out_ref):
        step = counter[0]
        counter[0] = step + 1
        place, head = (lax.div(step, kv_heads), lax.rem(step, kv_heads))
        for at, (payload, block) in enumerate(blocks):

            @pl.when((place == at) & (head == 0))
            def _():
                build_bias(at, payload, block)

        payload = payload_of(place)
        window = pl.ds(pl.multiple_of(block_of(place) * BLK + (lead - REACH), BLK), SPAN)
        lanes = pl.ds(pl.multiple_of(head * HEAD, HEAD), HEAD)
        key = kbuf[payload, window, lanes]
        value = vbuf[payload, window, lanes]
        for first in range(0, group, TOGETHER):
            heads = range(first, first + TOGETHER)
            query = jnp.concatenate([query_ref[0, :, g * HEAD : (g + 1) * HEAD] for g in heads], axis=0)
            scores = lax.dot_general(query, key, (((1,), (1,)), ((), ())), preferred_element_type=jnp.float32)
            scores = scores.reshape(TOGETHER, BLK, SPAN) + bias[place][None]
            top = jnp.max(scores, axis=-1, keepdims=True)
            weights = jnp.exp2((scores - top) * FACTOR)
            totals = jnp.sum(weights, axis=-1, keepdims=True)
            rounded = weights.astype(jnp.bfloat16).reshape(TOGETHER * BLK, SPAN)
            mixed = lax.dot_general(rounded, value, (((1,), (0,)), ((), ())), preferred_element_type=jnp.float32)
            mixed = (mixed.reshape(TOGETHER, BLK, HEAD) / totals).astype(jnp.bfloat16)
            for at, g in enumerate(heads):
                out_ref[:, g * HEAD : (g + 1) * HEAD] = mixed[at]

    pltpu.emit_pipeline(
        body,
        grid=(len(blocks), kv_heads),
        in_specs=[pl.BlockSpec((1, BLK, width), lambda i, h: (path_of(i), block_of(i), h))],
        out_specs=[pl.BlockSpec((BLK, width), lambda i, h: (i, h))],
    )(queries, out)
    for copy in packing:
        copy.wait()


def attend(blocks, operands, after=(), halo=None, pack=False):
    lengths, queries, keys, values, seg, par = operands
    rows, columns = queries.shape[1:]
    kv_heads = keys.shape[2] // HEAD
    held = rows + (REACH if halo else 0)
    out_shape = [jax.ShapeDtypeStruct((len(blocks) * BLK, columns), jnp.bfloat16)]
    out_specs = [ANY]
    if pack:
        out_shape.append(jax.ShapeDtypeStruct((2, 2, REACH, keys.shape[2]), jnp.bfloat16))
        out_shape.append(jax.ShapeDtypeStruct((2, 2, REACH), jnp.int32))
        out_specs += [ANY, VMEM]
    taken = 6 + (2 if halo else 0)

    def kernel(*refs):
        return attend_kernel(blocks, halo is not None, pack, *refs[:taken], *refs[taken + len(after) :])

    return pl.pallas_call(
        kernel,
        out_shape=out_shape,
        in_specs=[HBM] * 6 + ([ANY, VMEM] if halo else []) + [ANY] * len(after),
        out_specs=out_specs,
        scratch_shapes=[
            pltpu.VMEM((2, held, keys.shape[2]), jnp.bfloat16),
            pltpu.VMEM((2, held, keys.shape[2]), jnp.bfloat16),
            pltpu.VMEM((len(blocks), BLK, SPAN), jnp.float32),
            pltpu.VMEM(seg.shape, jnp.int32),
            pltpu.VMEM(par.shape, jnp.int32),
            pltpu.SMEM(lengths.shape, jnp.int32),
            pltpu.SMEM((1,), jnp.int32),
            pltpu.SemaphoreType.DMA((16,)),
        ]
        + ([pltpu.VMEM((2, 2, REACH, keys.shape[2]), jnp.bfloat16)] if pack else []),
        compiler_params=pltpu.CompilerParams(vmem_limit_bytes=VMEM_LIMIT),
        cost_estimate=COST,
    )(lengths, queries, keys, values, seg, par, *(halo or ()), *after)


def behind(value, *after):
    return pl.pallas_call(
        lambda *refs: None,
        out_shape=jax.ShapeDtypeStruct(value.shape, value.dtype),
        in_specs=[ANY] * (1 + len(after)),
        out_specs=ANY,
        input_output_aliases={0: 0},
        cost_estimate=COST,
    )(value, *after)


def place_kernel(held, aliased, *refs):
    pieces = refs[: len(held)]
    forward, back, stage, in_sems, out_sems = refs[len(held) + aliased :]
    place = lax.axis_index("pipe")
    even = lax.rem(place, 2) == 0
    edge = (place == 0) | (place == lax.axis_size("pipe") - 1)

    def go(kinds, even_here):
        moves = []
        for piece, (kind, blocks) in zip(pieces, held):
            if kind in kinds:
                target = forward if even_here == (kind != "swap") else back
                moves += [(piece, at, target, block) for at, block in enumerate(blocks)]
        loads = [
            pltpu.make_async_copy(piece.at[pl.ds(at * BLK, BLK)], stage.at[i], in_sems.at[i])
            for i, (piece, at, _, _) in enumerate(moves)
        ]
        stores = [
            pltpu.make_async_copy(stage.at[i], target.at[pl.ds(block * BLK, BLK)], out_sems.at[i])
            for i, (_, _, target, block) in enumerate(moves)
        ]
        for load in loads:
            load.start()
        for load, store in zip(loads, stores):
            load.wait()
            store.start()
        for store in stores:
            store.wait()

    for kinds, there in ((("swap", "own"), edge), (("swap", "far"), jnp.logical_not(edge))):
        if any(kind in kinds for kind, _ in held):
            for even_here in (True, False):

                @pl.when(there & (even == even_here))
                def _():
                    go(kinds, even_here)


def place(pieces, rows, outs=()):
    columns = pieces[0][1].shape[1]
    shape = jax.ShapeDtypeStruct((rows, columns), jnp.bfloat16)
    count = sum(len(blocks) for _, _, blocks in pieces)
    return pl.pallas_call(
        functools.partial(place_kernel, [(kind, blocks) for kind, _, blocks in pieces], len(outs)),
        out_shape=[shape, shape],
        in_specs=[ANY] * len(pieces) + [HBM] * len(outs),
        out_specs=[HBM, HBM],
        scratch_shapes=[
            pltpu.VMEM((count, BLK, columns), jnp.bfloat16),
            pltpu.SemaphoreType.DMA((count,)),
            pltpu.SemaphoreType.DMA((count,)),
        ],
        input_output_aliases={len(pieces) + i: i for i in range(len(outs))},
        compiler_params=pltpu.CompilerParams(vmem_limit_bytes=24 * 1024 * 1024),
        cost_estimate=COST,
    )(*(array for _, array, _ in pieces), *outs)


COST = pl.CostEstimate(flops=1024, bytes_accessed=1024, transcendentals=0)

SWAP = [(0, 1), (1, 0), (2, 3), (3, 2)]
DIAGONAL = [(1, 2), (2, 1)]
ACROSS = [(1, 3), (2, 0)]
ONWARD = [(3, 2), (0, 1)]


def on_device(queries, keys, values, segment, parent, tree_lengths):
    rows = queries.shape[2]
    operands = (tree_lengths[0], queries[0], keys[0], values[0], segment[0], parent[0])
    ring = [(source, source + 1) for source in range(lax.axis_size("dp") - 1)]

    swap_1, halo_kv, halo_info = attend([(0, 2), (0, 3)], operands, pack=True)
    got_1 = lax.ppermute(swap_1, "pipe", SWAP)
    halo = (lax.ppermute(halo_kv, "dp", ring), lax.ppermute(halo_info, "dp", ring))
    (routed_1,) = attend([(1, 2)], operands, after=(swap_1,))
    across_1 = lax.ppermute(routed_1, "pipe", ACROSS)
    (routed_2,) = attend([(1, 3)], operands, after=(routed_1,))
    across_2 = lax.ppermute(routed_2, "pipe", ACROSS)
    (swap_2,) = attend([(0, 0), (0, 1)], operands, after=(routed_2,), halo=halo)
    got_2 = lax.ppermute(swap_2, "pipe", SWAP)
    (direct,) = attend([(1, 0), (1, 1)], operands, after=(swap_2, got_1), halo=halo)
    diagonal = lax.ppermute(direct, "pipe", DIAGONAL)
    onward_1 = lax.ppermute(behind(across_1, direct), "pipe", ONWARD)
    onward_2 = lax.ppermute(behind(across_2, direct), "pipe", ONWARD)
    outs = place(
        [("swap", got_1, [2, 3]), ("own", direct, [0, 1]), ("own", routed_1, [2]), ("own", routed_2, [3])], rows
    )
    forward, back = place(
        [("swap", got_2, [0, 1]), ("far", diagonal, [0, 1]), ("far", onward_1, [2]), ("far", onward_2, [3])], rows, outs
    )
    return (forward[None], back[None])


def solution(mesh):
    return jax.shard_map(
        on_device,
        mesh=mesh,
        in_specs=(
            P("pipe", None, "dp", None),
            P("pipe", None, "dp", None),
            P("pipe", None, "dp", None),
            P("pipe", None, "dp"),
            P("pipe", None, "dp"),
            P("pipe", None, None),
        ),
        out_specs=(P("pipe", "dp", None), P("pipe", "dp", None)),
        check_vma=False,
    )
```

```python
import functools
import math

import jax
import jax.numpy as jnp
from jax import lax
from jax.experimental import pallas as pl
from jax.experimental.pallas import tpu as pltpu
from jax.sharding import PartitionSpec as P

BLK = 128
TREE_MOST = 3
KV_HEADS = 4
HEAD = 128
REACH = (TREE_MOST - 1) * BLK
SPAN = TREE_MOST * BLK
NEG = -1e30
FACTOR = math.log2(math.e) / math.sqrt(HEAD)

HALF = BLK // 2
CORNER = HALF + 16
INFO = 16
VMEM_LIMIT = 60 * 1024 * 1024

ANY = pl.BlockSpec(memory_space=pl.ANY)
HBM = pl.BlockSpec(memory_space=pltpu.HBM)


def flipped(array):
    count = array.shape[0]
    rows = lax.broadcasted_iota(jnp.int32, (count, count), 0)
    lanes = lax.broadcasted_iota(jnp.int32, (count, count), 1)
    swap = (rows + lanes == count - 1).astype(jnp.bfloat16)
    return jnp.dot(swap, array, preferred_element_type=jnp.float32).astype(jnp.bfloat16)


def stacked(array):
    return jnp.concatenate([array[:, at : at + HEAD] for at in range(0, array.shape[1], HEAD)], axis=0)


def product(left, right):
    return jnp.dot(left, right, preferred_element_type=jnp.float32)


def product_t(left, right):
    return lax.dot_general(left, right, (((1,), (1,)), ((), ())), preferred_element_type=jnp.float32)


def sides():
    lane = lax.broadcasted_iota(jnp.int32, (HALF, BLK), 1)
    gap = lax.broadcasted_iota(jnp.int32, (HALF, BLK), 0) + HALF
    return (lane < gap, lane > gap)


def plain_block(first, at):
    return at + (first <= at).astype(jnp.int32)


def attend_kernel(payload, groups, items, corner, pack, halo, *refs):
    heads = [head for group in groups for head in group]
    refs = list(refs)
    lengths_in, queries, keys, values, seg_in, par_in = refs[:6]
    refs = refs[6:]
    halo_in = refs.pop(0) if halo else None
    outs = [refs.pop(0) for _ in groups]
    pack_out = refs.pop(0) if pack else None
    kbuf, vbuf, bias, segs, pars, seg, par, lengths, marks, sems = refs[:10]
    refs = refs[10:]
    if halo:
        info = refs.pop(0)
    if corner:
        corner_q, corner_out = refs[:2]
        refs = refs[2:]
    if pack:
        packed = refs.pop(0)
    rows = keys.shape[1]
    kv_heads = keys.shape[2] // HEAD
    width = queries.shape[2] // kv_heads
    group = width // HEAD
    count = rows // BLK
    taken = len(heads)
    path = lax.rem(lax.axis_index("pipe"), 2)
    path = path if payload == 0 else 1 - path
    first_block = lax.axis_index("dp") * count
    lanes = pl.ds(heads[0] * HEAD, taken * HEAD)

    started = []

    def start(source, target):
        copy = pltpu.make_async_copy(source, target, sems.at[len(started)])
        copy.start()
        started.append(copy)
        return copy

    lengths_copy = start(lengths_in, lengths)
    row_copies = [start(seg_in, segs), start(par_in, pars)]
    kv_copies = []
    for which, (source, target) in enumerate(((keys, kbuf), (values, vbuf))):
        kv_copies.append(start(source.at[path, :, lanes], target.at[pl.ds(REACH, rows)]))
        if halo:
            kv_copies.append(start(halo_in.at[which, path, pl.ds(0, REACH), lanes], target.at[pl.ds(0, REACH)]))
    if halo:
        row_copies.append(start(halo_in.at[0, path, pl.ds(REACH, INFO)], info))
    pack_copies = []
    if pack:
        for each in range(2):
            for which, source in enumerate((keys, values)):
                source = source.at[each, pl.ds(rows - REACH, REACH)]
                pack_copies.append(start(source, packed.at[which, each, pl.ds(0, REACH)]))

    lengths_copy.wait()

    def step(entry, carry):
        end, begins = carry
        end = end + lengths[path, entry]
        return (end, tuple(jnp.where(end <= first_block + at, end, begin) for at, begin in enumerate(begins)))

    zero = jnp.int32(0)
    _, begins = lax.fori_loop(0, lengths.shape[1], step, (zero, (zero,) * count))
    first = jnp.int32(count - 1)
    for at in reversed(range(count)):
        marks[at] = begins[at]
        first = jnp.where(begins[at] == first_block + at, at, first)
    if corner:
        columns = pl.ds(heads[0] * width, taken * width)
        query_copy = start(queries.at[path, pl.ds(pl.multiple_of(first * BLK, BLK), BLK), columns], corner_q)

    for copy in row_copies:
        copy.wait()
    for source, target in ((segs, seg), (pars, par)):
        target[:, REACH:] = jnp.where(path == 0, source[0:1], source[1:2])
    if halo:
        numbers = info[...].astype(jnp.float32)
        seg[:, :REACH] = (numbers[0:1, :REACH] * 128.0 + numbers[1:2, :REACH]).astype(jnp.int32)
        par[:, :REACH] = (numbers[2:3, :REACH] * 128.0 + numbers[3:4, :REACH]).astype(jnp.int32)
    if pack:
        for each in range(2):
            at = lax.broadcasted_iota(jnp.int32, (INFO, REACH), 0)
            numbers = jnp.zeros((INFO, REACH), jnp.int32)
            for which, source in enumerate((segs, pars)):
                row = source[each : each + 1, rows - REACH :]
                numbers = jnp.where(at == 2 * which, row >> 7, numbers)
                numbers = jnp.where(at == 2 * which + 1, row & 127, numbers)
            numbers = numbers.astype(jnp.float32).astype(jnp.bfloat16)
            packed[0, each, REACH:, :REACH] = numbers
            packed[0, each, REACH:, REACH:] = jnp.zeros((INFO, keys.shape[2] - REACH), jnp.bfloat16)
            packed[1, each, REACH:, :] = jnp.zeros((INFO, keys.shape[2]), jnp.bfloat16)
        for copy in pack_copies:
            copy.wait()
        pack_store = start(packed, pack_out)
    for copy in kv_copies:
        copy.wait()

    def column(row):
        return jnp.transpose(jnp.broadcast_to(row, (BLK, BLK)))

    def related(block, back):
        ours = pl.ds(pl.multiple_of(REACH + block * BLK, BLK), BLK)
        theirs = pl.ds(pl.multiple_of(REACH + (block - back) * BLK, BLK), BLK)
        key_seg = seg[:, theirs]
        query_seg, query_par = (column(seg[:, ours]), column(par[:, ours]))
        found = (key_seg == query_seg) | (key_seg == query_par) | (par[:, theirs] == key_seg)
        if back:
            return found & (first_block + block - back >= marks[block])
        lane = lax.broadcasted_iota(jnp.int32, (BLK, BLK), 1)
        return found & (lane <= lax.broadcasted_iota(jnp.int32, (BLK, BLK), 0))

    if corner:
        query_copy.wait()
        seen = related(first, 0).astype(jnp.float32).astype(jnp.bfloat16)
        turned = jnp.transpose(flipped(jnp.transpose(flipped(seen[:HALF]).astype(jnp.float32)).astype(jnp.bfloat16)).astype(jnp.float32))
        low_bias = jnp.where(seen[HALF:].astype(jnp.float32) > 0.5, 0.0, NEG)
        high_bias = jnp.where(turned > 0.5, 0.0, NEG)
        own_rows = pl.ds(pl.multiple_of(REACH + first * BLK, BLK), BLK)
        left, right = sides()

        def shares(query, key, mask):
            scores = product_t(query, key).reshape(group, HALF, BLK) + mask[None]
            top = jnp.max(scores, axis=-1, keepdims=True)
            weights = jnp.exp2((scores - top) * FACTOR)
            return weights / jnp.sum(weights, axis=-1, keepdims=True)

        for at in range(taken):
            key = kbuf[own_rows, at * HEAD : (at + 1) * HEAD]
            query = corner_q[:, at * width : (at + 1) * width]
            low = shares(stacked(query[HALF:]), key, low_bias)
            high = shares(stacked(flipped(query[:HALF])), flipped(key), high_bias)
            mixed = jnp.where(right[None], high, first.astype(jnp.float32))
            mixed = jnp.where(left[None], low, mixed).astype(jnp.bfloat16)
            value = vbuf[own_rows, at * HEAD : (at + 1) * HEAD]
            for g in range(group):
                place = slice(at * width + g * HEAD, at * width + (g + 1) * HEAD)
                corner_out[:HALF, place] = mixed[g]
                corner_out[HALF:, place] = value[g * 16 : (g + 1) * 16]
        corner_stores = []
        for out, heads_here in zip(outs, groups):
            columns = pl.ds((heads_here[0] - heads[0]) * width, len(heads_here) * width)
            corner_stores.append(start(corner_out.at[:, columns], out.at[pl.ds(len(items) * BLK, CORNER)]))

    def block_of(place):
        at = jnp.int32(items[-1])
        for other in range(len(items) - 1):
            at = jnp.where(place == other, jnp.int32(items[other]), at)
        return at + (first <= at).astype(jnp.int32)

    def body(skipped, taken, query_ref, out_ref):
        step = marks[count]
        marks[count] = step + 1
        block, head = (block_of(lax.div(step, taken)), lax.rem(step, taken))

        @pl.when(head == 0)
        def _():
            for back in range(TREE_MOST):
                at = (TREE_MOST - 1 - back) * BLK
                bias[:, at : at + BLK] = jnp.where(related(block, back), 0.0, NEG)

        window = pl.ds(pl.multiple_of(block * BLK, BLK), SPAN)
        at = pl.ds(pl.multiple_of((skipped + head) * HEAD, HEAD), HEAD)
        scores = product_t(stacked(query_ref[0]), kbuf[window, at])
        scores = scores.reshape(group, BLK, SPAN) + bias[...][None]
        top = jnp.max(scores, axis=-1, keepdims=True)
        weights = jnp.exp2((scores - top) * FACTOR)
        totals = jnp.sum(weights, axis=-1, keepdims=True)
        rounded = weights.astype(jnp.bfloat16).reshape(group * BLK, SPAN)
        mixed = product(rounded, vbuf[window, at])
        mixed = (mixed.reshape(group, BLK, HEAD) / totals).astype(jnp.bfloat16)
        for g in range(group):
            out_ref[:, g * HEAD : (g + 1) * HEAD] = mixed[g]

    for out, heads_here in zip(outs, groups):
        if items:
            marks[count] = 0
            pltpu.emit_pipeline(
                functools.partial(body, heads_here[0] - heads[0], len(heads_here)),
                grid=(len(items), len(heads_here)),
                in_specs=[
                    pl.BlockSpec((1, BLK, width), lambda i, h, at=heads_here[0]: (path, block_of(i), at + h))
                ],
                out_specs=[pl.BlockSpec((BLK, width), lambda i, h: (i, h))],
            )(queries, out.at[pl.ds(0, len(items) * BLK)])
    if corner:
        for copy in corner_stores:
            copy.wait()
    if pack:
        pack_store.wait()


def attend(payload, groups, items, operands, after=(), halo=None, corner=False, pack=False):
    lengths, queries, keys, values, seg, par = operands
    rows, columns = queries.shape[1:]
    width = columns // (keys.shape[2] // HEAD)
    count = rows // BLK
    heads = [head for group in groups for head in group]
    height = len(items) * BLK + (CORNER if corner else 0)
    out_shape = [jax.ShapeDtypeStruct((height, len(group) * width), jnp.bfloat16) for group in groups]
    scratch = [
        pltpu.VMEM((REACH + rows, len(heads) * HEAD), jnp.bfloat16),
        pltpu.VMEM((REACH + rows, len(heads) * HEAD), jnp.bfloat16),
        pltpu.VMEM((BLK, SPAN), jnp.float32),
        pltpu.VMEM(seg.shape, jnp.int32),
        pltpu.VMEM(par.shape, jnp.int32),
        pltpu.VMEM((1, REACH + rows), jnp.int32),
        pltpu.VMEM((1, REACH + rows), jnp.int32),
        pltpu.SMEM(lengths.shape, jnp.int32),
        pltpu.SMEM((count + 1,), jnp.int32),
        pltpu.SemaphoreType.DMA((16,)),
    ]
    if halo is not None:
        scratch.append(pltpu.VMEM((INFO, keys.shape[2]), jnp.bfloat16))
    if corner:
        scratch.append(pltpu.VMEM((BLK, len(heads) * width), jnp.bfloat16))
        scratch.append(pltpu.VMEM((CORNER, len(heads) * width), jnp.bfloat16))
    if pack:
        packed = (2, 2, REACH + INFO, keys.shape[2])
        out_shape.append(jax.ShapeDtypeStruct(packed, jnp.bfloat16))
        scratch.append(pltpu.VMEM(packed, jnp.bfloat16))
    inputs = [lengths, queries, keys, values, seg, par] + ([] if halo is None else [halo])

    def kernel(*refs):
        refs = refs[: len(inputs)] + refs[len(inputs) + len(after) :]
        attend_kernel(payload, groups, items, corner, pack, halo is not None, *refs)

    return pl.pallas_call(
        kernel,
        out_shape=out_shape,
        in_specs=[HBM] * 6 + [ANY] * (len(inputs) - 6 + len(after)),
        out_specs=[ANY] * len(out_shape),
        scratch_shapes=scratch,
        compiler_params=pltpu.CompilerParams(vmem_limit_bytes=VMEM_LIMIT),
        cost_estimate=COST,
    )(*inputs, *after)


def behind(value, *after):
    return pl.pallas_call(
        lambda *refs: None,
        out_shape=jax.ShapeDtypeStruct(value.shape, value.dtype),
        in_specs=[ANY] * (1 + len(after)),
        out_specs=ANY,
        input_output_aliases={0: 0},
        cost_estimate=COST,
    )(value, *after)


def place_kernel(pieces, aliased, *refs):
    refs = list(refs)
    sources = [[refs.pop(0)] if swap else [refs.pop(0), refs.pop(0)] for swap, _, _, _ in pieces]
    refs = refs[aliased:]
    forward, back = refs[:2]
    stages, blocks = (refs[2 : 2 + len(pieces)], refs[2 + len(pieces) : 2 + 2 * len(pieces)])
    in_sems, out_sems = refs[2 + 2 * len(pieces) :]
    width = forward.shape[1] // KV_HEADS
    group = width // HEAD
    where = lax.axis_index("pipe")
    even = lax.rem(where, 2) == 0
    edge = (where == 0) | (where == lax.axis_size("pipe") - 1)

    for at, source in enumerate(sources):
        if len(source) == 1:
            pltpu.make_async_copy(source[0], stages[at], in_sems.at[at]).start()
        else:
            for own, mine in ((edge, source[1]), (jnp.logical_not(edge), source[0])):

                @pl.when(own)
                def _():
                    pltpu.make_async_copy(mine, stages[at], in_sems.at[at]).start()

    left, right = sides()
    first = {}
    stores = []
    for at, (swap, heads, items, corner) in enumerate(pieces):
        pltpu.make_async_copy(sources[at][0], stages[at], in_sems.at[at]).wait()
        stage = stages[at]
        top = len(items) * BLK
        if corner:
            tile = stage[top : top + 16, HALF : HALF + HEAD // 2].astype(jnp.float32)
            spot = (lax.broadcasted_iota(jnp.int32, tile.shape, 0) == 0) & (lax.broadcasted_iota(jnp.int32, tile.shape, 1) == 0)
            first[swap] = jnp.sum(jnp.where(spot, tile, 0.0)).astype(jnp.int32)
        columns = pl.ds(heads[0] * width, len(heads) * width)

        def store(source, block):
            rows = pl.ds(pl.multiple_of(block * BLK, BLK), BLK)
            for to_forward, target in ((even != swap, forward), (even == swap, back)):

                @pl.when(to_forward)
                def _():
                    pltpu.make_async_copy(source, target.at[rows, columns], out_sems.at[len(stores)]).start()

            stores.append(pltpu.make_async_copy(source, forward.at[rows, columns], out_sems.at[len(stores)]))

        for item, index in enumerate(items):
            store(stage.at[pl.ds(item * BLK, BLK)], plain_block(first[swap], index))
        if corner:
            for head in range(len(heads)):
                lanes = slice(head * width, (head + 1) * width)
                tiles = stage[top + HALF : top + CORNER, lanes]
                value = stacked(tiles)
                turned = flipped(value)
                shares = stage[top : top + HALF, lanes].astype(jnp.float32)
                shares = stacked(shares).reshape(group, HALF, BLK)

                def context(side, basis):
                    kept = jnp.where(side[None], shares, 0.0)
                    rest = 1.0 - jnp.sum(kept, axis=-1, keepdims=True)
                    mixed = product(kept.astype(jnp.bfloat16).reshape(group * HALF, BLK), basis)
                    mixed = mixed.reshape(group, HALF, HEAD) + rest * basis[HALF:].astype(jnp.float32)[None]
                    mixed = mixed.astype(jnp.bfloat16)
                    return jnp.concatenate([mixed[g] for g in range(group)], axis=1)

                blocks[at][HALF:, lanes] = context(left, value)
                blocks[at][:HALF, lanes] = flipped(context(right, turned))
            store(blocks[at], first[swap])
    for copy in stores:
        copy.wait()


def place(pieces, rows, outs=()):
    arrays = [array for piece in pieces for array in piece[0]]
    width = pieces[0][0][0].shape[1] // len(pieces[0][2])
    shape = jax.ShapeDtypeStruct((rows, width * KV_HEADS), jnp.bfloat16)
    held = [piece[0][0].shape for piece in pieces]
    return pl.pallas_call(
        functools.partial(place_kernel, [piece[1:] for piece in pieces], len(outs)),
        out_shape=[shape, shape],
        in_specs=[ANY] * len(arrays) + [HBM] * len(outs),
        out_specs=[HBM, HBM],
        scratch_shapes=[pltpu.VMEM(size, jnp.bfloat16) for size in held]
        + [pltpu.VMEM((BLK, size[1]), jnp.bfloat16) for size in held]
        + [pltpu.SemaphoreType.DMA((len(pieces),)), pltpu.SemaphoreType.DMA((4 * len(pieces),))],
        input_output_aliases={len(arrays) + i: i for i in range(len(outs))},
        compiler_params=pltpu.CompilerParams(vmem_limit_bytes=24 * 1024 * 1024),
        cost_estimate=COST,
    )(*arrays, *outs)


COST = pl.CostEstimate(flops=1024, bytes_accessed=1024, transcendentals=0)

SWAP = [(0, 1), (1, 0), (2, 3), (3, 2)]
DIAGONAL = [(1, 2), (2, 1)]
ACROSS = [(1, 3), (2, 0)]
ONWARD = [(3, 2), (0, 1)]


def on_device(queries, keys, values, segment, parent, tree_lengths):
    rows = queries.shape[2]
    operands = (tree_lengths[0], queries[0], keys[0], values[0], segment[0], parent[0])
    ring = [(source, source + 1) for source in range(lax.axis_size("dp") - 1)]
    every = tuple(range(KV_HEADS))

    corner, halo = attend(0, (every,), (), operands, corner=True, pack=True)
    got_0 = lax.ppermute(corner, "pipe", SWAP)
    halo = lax.ppermute(halo, "dp", ring)
    swap_1, swap_2 = attend(0, ((0, 1), (2, 3)), (2,), operands, after=(corner,))
    got_1 = lax.ppermute(swap_1, "pipe", SWAP)
    got_2 = lax.ppermute(swap_2, "pipe", SWAP)
    (swap_3,) = attend(0, (every,), (0, 1), operands, after=(swap_1,), halo=halo)
    got_3 = lax.ppermute(swap_3, "pipe", SWAP)
    routed_1, routed_2 = attend(1, ((0,), (1,)), (0, 1, 2), operands, after=(swap_3,), halo=halo, corner=True)
    across_1 = lax.ppermute(routed_1, "pipe", ACROSS)
    across_2 = lax.ppermute(routed_2, "pipe", ACROSS)
    (direct,) = attend(
        1, ((2, 3),), (0, 1, 2), operands, after=(routed_1, got_0, got_1, got_2), halo=halo, corner=True
    )
    diagonal = lax.ppermute(direct, "pipe", DIAGONAL)
    onward_1 = lax.ppermute(behind(across_1, direct), "pipe", ONWARD)
    onward_2 = lax.ppermute(behind(across_2, direct), "pipe", ONWARD)
    outs = place(
        [
            ((got_0,), True, every, (), True),
            ((got_1,), True, (0, 1), (2,), False),
            ((got_2,), True, (2, 3), (2,), False),
            ((got_3,), True, every, (0, 1), False),
        ],
        rows,
    )
    forward, back = place(
        [
            ((onward_1, routed_1), False, (0,), (0, 1, 2), True),
            ((onward_2, routed_2), False, (1,), (0, 1, 2), True),
            ((diagonal, direct), False, (2, 3), (0, 1, 2), True),
        ],
        rows,
        outs,
    )
    return (forward[None], back[None])


def solution(mesh):
    return jax.shard_map(
        on_device,
        mesh=mesh,
        in_specs=(
            P("pipe", None, "dp", None),
            P("pipe", None, "dp", None),
            P("pipe", None, "dp", None),
            P("pipe", None, "dp"),
            P("pipe", None, "dp"),
            P("pipe", None, None),
        ),
        out_specs=(P("pipe", "dp", None), P("pipe", "dp", None)),
        check_vma=False,
    )
```

```python
import functools
import math

import jax
import jax.numpy as jnp
from jax import lax
from jax.experimental import pallas as pl
from jax.experimental.pallas import tpu as pltpu
from jax.sharding import PartitionSpec as P

BLK = 128
TREE_MOST = 3
KV_HEADS = 4
HEAD = 128
REACH = (TREE_MOST - 1) * BLK
SPAN = TREE_MOST * BLK
NEG = -1e30
FACTOR = math.log2(math.e) / math.sqrt(HEAD)

HALF = BLK // 2
CORNER = HALF + 16
INFO = 16
VMEM_LIMIT = 60 * 1024 * 1024

ANY = pl.BlockSpec(memory_space=pl.ANY)
HBM = pl.BlockSpec(memory_space=pltpu.HBM)


def flipped(array):
    count = array.shape[0]
    rows = lax.broadcasted_iota(jnp.int32, (count, count), 0)
    lanes = lax.broadcasted_iota(jnp.int32, (count, count), 1)
    swap = (rows + lanes == count - 1).astype(jnp.bfloat16)
    return jnp.dot(swap, array, preferred_element_type=jnp.float32).astype(jnp.bfloat16)


def stacked(array):
    return jnp.concatenate([array[:, at : at + HEAD] for at in range(0, array.shape[1], HEAD)], axis=0)


def product(left, right):
    return jnp.dot(left, right, preferred_element_type=jnp.float32)


def product_t(left, right):
    return lax.dot_general(left, right, (((1,), (1,)), ((), ())), preferred_element_type=jnp.float32)


def sides():
    lane = lax.broadcasted_iota(jnp.int32, (HALF, BLK), 1)
    gap = lax.broadcasted_iota(jnp.int32, (HALF, BLK), 0) + HALF
    return (lane < gap, lane > gap)


def plain_block(first, at):
    return at + (first <= at).astype(jnp.int32)


def attend_kernel(payload, groups, items, corner, pack, halo, *refs):
    heads = [head for group in groups for head in group]
    refs = list(refs)
    lengths_in, queries, keys, values, seg_in, par_in = refs[:6]
    refs = refs[6:]
    halo_in = refs.pop(0) if halo else None
    outs = [refs.pop(0) for _ in groups]
    pack_outs = [refs.pop(0), refs.pop(0)] if pack else None
    kbuf, vbuf, bias, segs, pars, seg, par, lengths, marks, sems = refs[:10]
    refs = refs[10:]
    if halo:
        info = refs.pop(0)
    if corner:
        corner_q, corner_out = refs[:2]
        refs = refs[2:]
    if pack:
        packed = refs.pop(0)
    rows = keys.shape[1]
    kv_heads = keys.shape[2] // HEAD
    width = queries.shape[2] // kv_heads
    group = width // HEAD
    count = rows // BLK
    taken = len(heads)
    path = lax.rem(lax.axis_index("pipe"), 2)
    path = path if payload == 0 else 1 - path
    first_block = lax.axis_index("dp") * count
    lanes = pl.ds(heads[0] * HEAD, taken * HEAD)

    started = []

    def start(source, target):
        copy = pltpu.make_async_copy(source, target, sems.at[len(started)])
        copy.start()
        started.append(copy)
        return copy

    lengths_copy = start(lengths_in, lengths)
    row_copies = [start(seg_in, segs), start(par_in, pars)]
    kv_copies = []
    for which, (source, target) in enumerate(((keys, kbuf), (values, vbuf))):
        kv_copies.append(start(source.at[path, :, lanes], target.at[pl.ds(REACH, rows)]))
        if halo:
            kv_copies.append(start(halo_in.at[which, pl.ds(0, REACH), lanes], target.at[pl.ds(0, REACH)]))
    if halo:
        row_copies.append(start(halo_in.at[0, pl.ds(REACH, INFO)], info))
    pack_copies = []
    if pack:
        for each in range(2):
            for which, source in enumerate((keys, values)):
                source = source.at[each, pl.ds(rows - REACH, REACH)]
                pack_copies.append(start(source, packed.at[each, which, pl.ds(0, REACH)]))

    lengths_copy.wait()

    def step(entry, carry):
        end, begins = carry
        end = end + lengths[path, entry]
        return (end, tuple(jnp.where(end <= first_block + at, end, begin) for at, begin in enumerate(begins)))

    zero = jnp.int32(0)
    _, begins = lax.fori_loop(0, lengths.shape[1], step, (zero, (zero,) * count), unroll=8)
    first = jnp.int32(TREE_MOST - 1)
    for at in reversed(range(count)):
        marks[at] = begins[at]
        if at < TREE_MOST - 1:
            first = jnp.where(begins[at] == first_block + at, at, first)
    if corner:
        columns = pl.ds(heads[0] * width, taken * width)
        query_copy = start(queries.at[path, pl.ds(pl.multiple_of(first * BLK, BLK), BLK), columns], corner_q)

    def rows_ready():
        for copy in row_copies:
            copy.wait()
        for source, target in ((segs, seg), (pars, par)):
            target[:, REACH:] = jnp.where(path == 0, source[0:1], source[1:2])
        if halo:
            numbers = info[...].astype(jnp.float32)
            seg[:, :REACH] = (numbers[0:1, :REACH] * 128.0 + numbers[1:2, :REACH]).astype(jnp.int32)
            par[:, :REACH] = (numbers[2:3, :REACH] * 128.0 + numbers[3:4, :REACH]).astype(jnp.int32)
        for copy in kv_copies:
            copy.wait()

    if corner:
        rows_ready()
    if pack:
        for each in range(2):
            at = lax.broadcasted_iota(jnp.int32, (INFO, REACH), 0)
            numbers = jnp.zeros((INFO, REACH), jnp.int32)
            for which, source in enumerate((segs, pars)):
                row = source[each : each + 1, rows - REACH :]
                numbers = jnp.where(at == 2 * which, row >> 7, numbers)
                numbers = jnp.where(at == 2 * which + 1, row & 127, numbers)
            numbers = numbers.astype(jnp.float32).astype(jnp.bfloat16)
            packed[each, 0, REACH:, :REACH] = numbers
            packed[each, 0, REACH:, REACH:] = jnp.zeros((INFO, keys.shape[2] - REACH), jnp.bfloat16)
            packed[each, 1, REACH:, :] = jnp.zeros((INFO, keys.shape[2]), jnp.bfloat16)
        for copy in pack_copies:
            copy.wait()
        pack_stores = [start(packed.at[path], pack_outs[0]), start(packed.at[1 - path], pack_outs[1])]

    def column(row):
        return jnp.transpose(jnp.broadcast_to(row, (BLK, BLK)))

    def related(block, back):
        ours = pl.ds(pl.multiple_of(REACH + block * BLK, BLK), BLK)
        theirs = pl.ds(pl.multiple_of(REACH + (block - back) * BLK, BLK), BLK)
        key_seg = seg[:, theirs]
        query_seg, query_par = (column(seg[:, ours]), column(par[:, ours]))
        found = (key_seg == query_seg) | (key_seg == query_par) | (par[:, theirs] == key_seg)
        if back:
            return found & (first_block + block - back >= marks[block])
        lane = lax.broadcasted_iota(jnp.int32, (BLK, BLK), 1)
        return found & (lane <= lax.broadcasted_iota(jnp.int32, (BLK, BLK), 0))

    if corner:
        query_copy.wait()
        seen = related(first, 0).astype(jnp.float32).astype(jnp.bfloat16)
        turned = jnp.transpose(flipped(jnp.transpose(flipped(seen[:HALF]).astype(jnp.float32)).astype(jnp.bfloat16)).astype(jnp.float32))
        low_bias = jnp.where(seen[HALF:].astype(jnp.float32) > 0.5, 0.0, NEG)
        high_bias = jnp.where(turned > 0.5, 0.0, NEG)
        own_rows = pl.ds(pl.multiple_of(REACH + first * BLK, BLK), BLK)
        left, right = sides()

        def shares(query, key, mask):
            scores = product_t(query, key).reshape(group, HALF, BLK) + mask[None]
            top = jnp.max(scores, axis=-1, keepdims=True)
            weights = jnp.exp2((scores - top) * FACTOR)
            return weights / jnp.sum(weights, axis=-1, keepdims=True)

        for at in range(taken):
            key = kbuf[own_rows, at * HEAD : (at + 1) * HEAD]
            query = corner_q[:, at * width : (at + 1) * width]
            low = shares(stacked(query[HALF:]), key, low_bias)
            high = shares(stacked(flipped(query[:HALF])), flipped(key), high_bias)
            mixed = jnp.where(right[None], high, first.astype(jnp.float32))
            mixed = jnp.where(left[None], low, mixed).astype(jnp.bfloat16)
            value = vbuf[own_rows, at * HEAD : (at + 1) * HEAD]
            for g in range(group):
                place = slice(at * width + g * HEAD, at * width + (g + 1) * HEAD)
                corner_out[:HALF, place] = mixed[g]
                corner_out[HALF:, place] = value[g * 16 : (g + 1) * 16]
        corner_stores = []
        for out, heads_here in zip(outs, groups):
            columns = pl.ds((heads_here[0] - heads[0]) * width, len(heads_here) * width)
            corner_stores.append(start(corner_out.at[:, columns], out.at[pl.ds(len(items) * BLK, CORNER)]))

    def block_of(place):
        at = jnp.int32(items[-1])
        for other in range(len(items) - 1):
            at = jnp.where(place == other, jnp.int32(items[other]), at)
        if min(items) >= TREE_MOST - 1:
            return at + 1
        return at + (first <= at).astype(jnp.int32)

    def body(skipped, taken, query_ref, out_ref):
        step = marks[count]
        marks[count] = step + 1
        block, head = (block_of(lax.div(step, taken)), lax.rem(step, taken))

        if not corner:
            pl.when(step == 0)(rows_ready)

        @pl.when(head == 0)
        def _():
            for back in range(TREE_MOST):
                at = (TREE_MOST - 1 - back) * BLK
                bias[:, at : at + BLK] = jnp.where(related(block, back), 0.0, NEG)

        window = pl.ds(pl.multiple_of(block * BLK, BLK), SPAN)
        at = pl.ds(pl.multiple_of((skipped + head) * HEAD, HEAD), HEAD)
        scores = product_t(stacked(query_ref[0]), kbuf[window, at])
        scores = scores.reshape(group, BLK, SPAN) + bias[...][None]
        top = jnp.max(scores, axis=-1, keepdims=True)
        weights = jnp.exp2((scores - top) * FACTOR)
        totals = jnp.sum(weights, axis=-1, keepdims=True)
        rounded = weights.astype(jnp.bfloat16).reshape(group * BLK, SPAN)
        mixed = product(rounded, vbuf[window, at])
        mixed = (mixed.reshape(group, BLK, HEAD) / totals).astype(jnp.bfloat16)
        for g in range(group):
            out_ref[:, g * HEAD : (g + 1) * HEAD] = mixed[g]

    for out, heads_here in zip(outs, groups):
        if items:
            marks[count] = 0
            pltpu.emit_pipeline(
                functools.partial(body, heads_here[0] - heads[0], len(heads_here)),
                grid=(len(items), len(heads_here)),
                in_specs=[
                    pl.BlockSpec((1, BLK, width), lambda i, h, at=heads_here[0]: (path, block_of(i), at + h))
                ],
                out_specs=[pl.BlockSpec((BLK, width), lambda i, h: (i, h))],
            )(queries, out.at[pl.ds(0, len(items) * BLK)])
    if corner:
        for copy in corner_stores:
            copy.wait()
    if pack:
        for copy in pack_stores:
            copy.wait()


def attend(payload, groups, items, operands, after=(), halo=None, corner=False, pack=False):
    lengths, queries, keys, values, seg, par = operands
    rows, columns = queries.shape[1:]
    width = columns // (keys.shape[2] // HEAD)
    count = rows // BLK
    heads = [head for group in groups for head in group]
    height = len(items) * BLK + (CORNER if corner else 0)
    out_shape = [jax.ShapeDtypeStruct((height, len(group) * width), jnp.bfloat16) for group in groups]
    scratch = [
        pltpu.VMEM((REACH + rows, len(heads) * HEAD), jnp.bfloat16),
        pltpu.VMEM((REACH + rows, len(heads) * HEAD), jnp.bfloat16),
        pltpu.VMEM((BLK, SPAN), jnp.float32),
        pltpu.VMEM(seg.shape, jnp.int32),
        pltpu.VMEM(par.shape, jnp.int32),
        pltpu.VMEM((1, REACH + rows), jnp.int32),
        pltpu.VMEM((1, REACH + rows), jnp.int32),
        pltpu.SMEM(lengths.shape, jnp.int32),
        pltpu.SMEM((count + 1,), jnp.int32),
        pltpu.SemaphoreType.DMA((16,)),
    ]
    if halo is not None:
        scratch.append(pltpu.VMEM((INFO, keys.shape[2]), jnp.bfloat16))
    if corner:
        scratch.append(pltpu.VMEM((BLK, len(heads) * width), jnp.bfloat16))
        scratch.append(pltpu.VMEM((CORNER, len(heads) * width), jnp.bfloat16))
    if pack:
        packed = (2, 2, REACH + INFO, keys.shape[2])
        out_shape += [jax.ShapeDtypeStruct(packed[1:], jnp.bfloat16)] * 2
        scratch.append(pltpu.VMEM(packed, jnp.bfloat16))
    inputs = [lengths, queries, keys, values, seg, par] + ([] if halo is None else [halo])

    def kernel(*refs):
        refs = refs[: len(inputs)] + refs[len(inputs) + len(after) :]
        attend_kernel(payload, groups, items, corner, pack, halo is not None, *refs)

    return pl.pallas_call(
        kernel,
        out_shape=out_shape,
        in_specs=[HBM] * 6 + [ANY] * (len(inputs) - 6 + len(after)),
        out_specs=[ANY] * len(out_shape),
        scratch_shapes=scratch,
        compiler_params=pltpu.CompilerParams(vmem_limit_bytes=VMEM_LIMIT),
        cost_estimate=COST,
    )(*inputs, *after)


def behind(value, *after):
    return pl.pallas_call(
        lambda *refs: None,
        out_shape=jax.ShapeDtypeStruct(value.shape, value.dtype),
        in_specs=[ANY] * (1 + len(after)),
        out_specs=ANY,
        input_output_aliases={0: 0},
        cost_estimate=COST,
    )(value, *after)


def place_kernel(pieces, aliased, *refs):
    refs = list(refs)
    sources = [[refs.pop(0)] if swap else [refs.pop(0), refs.pop(0)] for swap, _, _, _ in pieces]
    refs = refs[aliased:]
    forward, back = refs[:2]
    stages, blocks = (refs[2 : 2 + len(pieces)], refs[2 + len(pieces) : 2 + 2 * len(pieces)])
    in_sems, out_sems = refs[2 + 2 * len(pieces) :]
    width = forward.shape[1] // KV_HEADS
    group = width // HEAD
    where = lax.axis_index("pipe")
    even = lax.rem(where, 2) == 0
    edge = (where == 0) | (where == lax.axis_size("pipe") - 1)

    for at, source in enumerate(sources):
        if len(source) == 1:
            pltpu.make_async_copy(source[0], stages[at], in_sems.at[at]).start()
        else:
            for own, mine in ((edge, source[1]), (jnp.logical_not(edge), source[0])):

                @pl.when(own)
                def _():
                    pltpu.make_async_copy(mine, stages[at], in_sems.at[at]).start()

    left, right = sides()
    first = {}
    stores = []
    for at, (swap, heads, items, corner) in enumerate(pieces):
        pltpu.make_async_copy(sources[at][0], stages[at], in_sems.at[at]).wait()
        stage = stages[at]
        top = len(items) * BLK
        if corner:
            tile = stage[top : top + 16, HALF : HALF + HEAD // 2].astype(jnp.float32)
            spot = (lax.broadcasted_iota(jnp.int32, tile.shape, 0) == 0) & (lax.broadcasted_iota(jnp.int32, tile.shape, 1) == 0)
            first[swap] = jnp.sum(jnp.where(spot, tile, 0.0)).astype(jnp.int32)
        columns = pl.ds(heads[0] * width, len(heads) * width)

        def store(source, block):
            rows = pl.ds(pl.multiple_of(block * BLK, BLK), BLK)
            for to_forward, target in ((even != swap, forward), (even == swap, back)):

                @pl.when(to_forward)
                def _():
                    pltpu.make_async_copy(source, target.at[rows, columns], out_sems.at[len(stores)]).start()

            stores.append(pltpu.make_async_copy(source, forward.at[rows, columns], out_sems.at[len(stores)]))

        for item, index in enumerate(items):
            store(stage.at[pl.ds(item * BLK, BLK)], plain_block(first[swap], index))
        if corner:
            for head in range(len(heads)):
                lanes = slice(head * width, (head + 1) * width)
                tiles = stage[top + HALF : top + CORNER, lanes]
                value = stacked(tiles)
                turned = flipped(value)
                shares = stage[top : top + HALF, lanes].astype(jnp.float32)
                shares = stacked(shares).reshape(group, HALF, BLK)

                def context(side, basis):
                    kept = jnp.where(side[None], shares, 0.0)
                    rest = 1.0 - jnp.sum(kept, axis=-1, keepdims=True)
                    mixed = product(kept.astype(jnp.bfloat16).reshape(group * HALF, BLK), basis)
                    mixed = mixed.reshape(group, HALF, HEAD) + rest * basis[HALF:].astype(jnp.float32)[None]
                    mixed = mixed.astype(jnp.bfloat16)
                    return jnp.concatenate([mixed[g] for g in range(group)], axis=1)

                blocks[at][HALF:, lanes] = context(left, value)
                blocks[at][:HALF, lanes] = flipped(context(right, turned))
            store(blocks[at], first[swap])
    for copy in stores:
        copy.wait()


def place(pieces, rows, outs=()):
    arrays = [array for piece in pieces for array in piece[0]]
    width = pieces[0][0][0].shape[1] // len(pieces[0][2])
    shape = jax.ShapeDtypeStruct((rows, width * KV_HEADS), jnp.bfloat16)
    held = [piece[0][0].shape for piece in pieces]
    return pl.pallas_call(
        functools.partial(place_kernel, [piece[1:] for piece in pieces], len(outs)),
        out_shape=[shape, shape],
        in_specs=[ANY] * len(arrays) + [HBM] * len(outs),
        out_specs=[HBM, HBM],
        scratch_shapes=[pltpu.VMEM(size, jnp.bfloat16) for size in held]
        + [pltpu.VMEM((BLK, size[1]), jnp.bfloat16) for size in held]
        + [pltpu.SemaphoreType.DMA((len(pieces),)), pltpu.SemaphoreType.DMA((4 * len(pieces),))],
        input_output_aliases={len(arrays) + i: i for i in range(len(outs))},
        compiler_params=pltpu.CompilerParams(vmem_limit_bytes=24 * 1024 * 1024),
        cost_estimate=COST,
    )(*arrays, *outs)


COST = pl.CostEstimate(flops=1024, bytes_accessed=1024, transcendentals=0)

SWAP = [(0, 1), (1, 0), (2, 3), (3, 2)]
DIAGONAL = [(1, 2), (2, 1)]
ACROSS = [(1, 3), (2, 0)]
ONWARD = [(3, 2), (0, 1)]


def on_device(queries, keys, values, segment, parent, tree_lengths):
    rows = queries.shape[2]
    operands = (tree_lengths[0], queries[0], keys[0], values[0], segment[0], parent[0])
    ring = [(source, source + 1) for source in range(lax.axis_size("dp") - 1)]
    every = tuple(range(KV_HEADS))

    (swap_0,) = attend(0, ((0,),), (2,), operands)
    got_0 = lax.ppermute(swap_0, "pipe", SWAP)
    (swap_1,) = attend(0, ((1, 2, 3),), (2,), operands, after=(swap_0,))
    got_1 = lax.ppermute(swap_1, "pipe", SWAP)
    corner, halo, far_halo = attend(0, (every,), (), operands, after=(swap_1, got_0), corner=True, pack=True)
    got_corner = lax.ppermute(corner, "pipe", SWAP)
    halo = lax.ppermute(halo, "dp", ring)
    far_halo = lax.ppermute(far_halo, "dp", ring)
    (swap_2,) = attend(0, (every,), (0, 1), operands, after=(corner,), halo=halo)
    got_2 = lax.ppermute(swap_2, "pipe", SWAP)
    routed_1, routed_2 = attend(1, ((0,), (1,)), (0, 1, 2), operands, after=(swap_2,), halo=far_halo, corner=True)
    across_1 = lax.ppermute(routed_1, "pipe", ACROSS)
    direct_1, direct_2 = attend(
        1, ((2,), (3,)), (0, 1, 2), operands, after=(routed_1, got_1, got_corner), halo=far_halo, corner=True
    )
    diagonal_1 = lax.ppermute(direct_1, "pipe", DIAGONAL)
    across_2 = lax.ppermute(behind(routed_2, direct_1), "pipe", ACROSS)
    diagonal_2 = lax.ppermute(behind(direct_2, across_2), "pipe", DIAGONAL)
    onward_1 = lax.ppermute(behind(across_1, direct_1), "pipe", ONWARD)
    onward_2 = lax.ppermute(behind(across_2, direct_1), "pipe", ONWARD)
    outs = place(
        [
            ((got_corner,), True, every, (), True),
            ((got_0,), True, (0,), (2,), False),
            ((got_1,), True, (1, 2, 3), (2,), False),
            ((got_2,), True, every, (0, 1), False),
        ],
        rows,
    )
    outs = place(
        [
            ((onward_1, routed_1), False, (0,), (0, 1, 2), True),
            ((diagonal_1, direct_1), False, (2,), (0, 1, 2), True),
        ],
        rows,
        outs,
    )
    forward, back = place(
        [
            ((onward_2, routed_2), False, (1,), (0, 1, 2), True),
            ((diagonal_2, direct_2), False, (3,), (0, 1, 2), True),
        ],
        rows,
        outs,
    )
    return (forward[None], back[None])


def solution(mesh):
    return jax.shard_map(
        on_device,
        mesh=mesh,
        in_specs=(
            P("pipe", None, "dp", None),
            P("pipe", None, "dp", None),
            P("pipe", None, "dp", None),
            P("pipe", None, "dp"),
            P("pipe", None, "dp"),
            P("pipe", None, None),
        ),
        out_specs=(P("pipe", "dp", None), P("pipe", "dp", None)),
        check_vma=False,
    )
```

```python
import functools
import math

import jax
import jax.numpy as jnp
from jax import lax
from jax.experimental import pallas as pl
from jax.experimental.pallas import tpu as pltpu
from jax.sharding import PartitionSpec as P

BLK = 128
TREE_MOST = 3
KV_HEADS = 4
HEAD = 128
REACH = (TREE_MOST - 1) * BLK
SPAN = TREE_MOST * BLK
NEG = -1e30
FACTOR = math.log2(math.e) / math.sqrt(HEAD)

HALF = BLK // 2
CORNER = HALF + 16
INFO = 16
VMEM_LIMIT = 60 * 1024 * 1024

ANY = pl.BlockSpec(memory_space=pl.ANY)
HBM = pl.BlockSpec(memory_space=pltpu.HBM)


def flipped(array):
    count = array.shape[0]
    rows = lax.broadcasted_iota(jnp.int32, (count, count), 0)
    lanes = lax.broadcasted_iota(jnp.int32, (count, count), 1)
    swap = (rows + lanes == count - 1).astype(jnp.bfloat16)
    return jnp.dot(swap, array, preferred_element_type=jnp.float32).astype(jnp.bfloat16)


def stacked(array):
    return jnp.concatenate([array[:, at : at + HEAD] for at in range(0, array.shape[1], HEAD)], axis=0)


def product(left, right):
    return jnp.dot(left, right, preferred_element_type=jnp.float32)


def product_t(left, right):
    return lax.dot_general(left, right, (((1,), (1,)), ((), ())), preferred_element_type=jnp.float32)


def sides():
    lane = lax.broadcasted_iota(jnp.int32, (HALF, BLK), 1)
    gap = lax.broadcasted_iota(jnp.int32, (HALF, BLK), 0) + HALF
    return (lane < gap, lane > gap)


def plain_block(first, at):
    return at + (first <= at).astype(jnp.int32)


def attend_kernel(payload, groups, items, corner, pack, halo, last, *refs):
    heads = [head for group in groups for head in group]
    refs = list(refs)
    lengths_in, queries, keys, values, seg_in, par_in = refs[:6]
    refs = refs[6:]
    halo_in = refs.pop(0) if halo else None
    outs = [refs.pop(0) for _ in groups]
    pack_outs = [refs.pop(0), refs.pop(0)] if pack else None
    kbuf, vbuf, bias, segs, pars, seg, par, lengths, marks, sems = refs[:10]
    refs = refs[10:]
    if halo:
        info = refs.pop(0)
    if corner:
        corner_q, corner_out = refs[:2]
        refs = refs[2:]
    if pack:
        packed = refs.pop(0)
    if last:
        last_q, last_out = refs[:2]
    rows = keys.shape[1]
    kv_heads = keys.shape[2] // HEAD
    width = queries.shape[2] // kv_heads
    group = width // HEAD
    count = rows // BLK
    taken = len(heads)
    path = lax.rem(lax.axis_index("pipe"), 2)
    path = path if payload == 0 else 1 - path
    first_block = lax.axis_index("dp") * count
    lanes = pl.ds(heads[0] * HEAD, taken * HEAD)

    started = []

    def start(source, target):
        copy = pltpu.make_async_copy(source, target, sems.at[len(started)])
        copy.start()
        started.append(copy)
        return copy

    lengths_copy = start(lengths_in, lengths)
    row_copies = [start(seg_in, segs), start(par_in, pars)]
    query_copies = []
    if last:
        for at, head in enumerate(heads):
            source = queries.at[path, pl.ds(TREE_MOST * BLK, BLK), pl.ds(head * width, width)]
            query_copies.append(start(source, last_q.at[:, pl.ds(at * width, width)]))
    kv_copies = []
    for which, (source, target) in enumerate(((keys, kbuf), (values, vbuf))):
        kv_copies.append(start(source.at[path, :, lanes], target.at[pl.ds(REACH, rows)]))
        if halo:
            kv_copies.append(start(halo_in.at[which, pl.ds(0, REACH), lanes], target.at[pl.ds(0, REACH)]))
    if halo:
        row_copies.append(start(halo_in.at[0, pl.ds(REACH, INFO)], info))
    pack_copies = []
    if pack:
        for each in range(2):
            for which, source in enumerate((keys, values)):
                source = source.at[each, pl.ds(rows - REACH, REACH)]
                pack_copies.append(start(source, packed.at[each, which, pl.ds(0, REACH)]))

    lengths_copy.wait()

    def step(entry, carry):
        end, begins = carry
        end = end + lengths[path, entry]
        return (end, tuple(jnp.where(end <= first_block + at, end, begin) for at, begin in enumerate(begins)))

    zero = jnp.int32(0)
    _, begins = lax.fori_loop(0, lengths.shape[1], step, (zero, (zero,) * count), unroll=8)
    first = jnp.int32(TREE_MOST - 1)
    for at in reversed(range(count)):
        marks[at] = begins[at]
        if at < TREE_MOST - 1:
            first = jnp.where(begins[at] == first_block + at, at, first)
    if corner:
        columns = pl.ds(heads[0] * width, taken * width)
        query_copy = start(queries.at[path, pl.ds(pl.multiple_of(first * BLK, BLK), BLK), columns], corner_q)

    def rows_ready():
        for copy in row_copies:
            copy.wait()
        for source, target in ((segs, seg), (pars, par)):
            target[:, REACH:] = jnp.where(path == 0, source[0:1], source[1:2])
        if halo:
            numbers = info[...].astype(jnp.float32)
            seg[:, :REACH] = (numbers[0:1, :REACH] * 128.0 + numbers[1:2, :REACH]).astype(jnp.int32)
            par[:, :REACH] = (numbers[2:3, :REACH] * 128.0 + numbers[3:4, :REACH]).astype(jnp.int32)

    def all_ready():
        rows_ready()
        for copy in kv_copies:
            copy.wait()

    if corner:
        all_ready()
    if pack:
        for each in range(2):
            at = lax.broadcasted_iota(jnp.int32, (INFO, REACH), 0)
            numbers = jnp.zeros((INFO, REACH), jnp.int32)
            for which, source in enumerate((segs, pars)):
                row = source[each : each + 1, rows - REACH :]
                numbers = jnp.where(at == 2 * which, row >> 7, numbers)
                numbers = jnp.where(at == 2 * which + 1, row & 127, numbers)
            numbers = numbers.astype(jnp.float32).astype(jnp.bfloat16)
            packed[each, 0, REACH:, :REACH] = numbers
            packed[each, 0, REACH:, REACH:] = jnp.zeros((INFO, keys.shape[2] - REACH), jnp.bfloat16)
            packed[each, 1, REACH:, :] = jnp.zeros((INFO, keys.shape[2]), jnp.bfloat16)
        for copy in pack_copies:
            copy.wait()
        pack_stores = [start(packed.at[path], pack_outs[0]), start(packed.at[1 - path], pack_outs[1])]

    def column(row):
        return jnp.transpose(jnp.broadcast_to(row, (BLK, BLK)))

    def related(block, back):
        ours = pl.ds(pl.multiple_of(REACH + block * BLK, BLK), BLK)
        theirs = pl.ds(pl.multiple_of(REACH + (block - back) * BLK, BLK), BLK)
        key_seg = seg[:, theirs]
        query_seg, query_par = (column(seg[:, ours]), column(par[:, ours]))
        found = (key_seg == query_seg) | (key_seg == query_par) | (par[:, theirs] == key_seg)
        if back:
            return found & (first_block + block - back >= marks[block])
        lane = lax.broadcasted_iota(jnp.int32, (BLK, BLK), 1)
        return found & (lane <= lax.broadcasted_iota(jnp.int32, (BLK, BLK), 0))

    if corner:
        query_copy.wait()
        seen = related(first, 0).astype(jnp.float32).astype(jnp.bfloat16)
        turned = jnp.transpose(flipped(jnp.transpose(flipped(seen[:HALF]).astype(jnp.float32)).astype(jnp.bfloat16)).astype(jnp.float32))
        low_bias = jnp.where(seen[HALF:].astype(jnp.float32) > 0.5, 0.0, NEG)
        high_bias = jnp.where(turned > 0.5, 0.0, NEG)
        own_rows = pl.ds(pl.multiple_of(REACH + first * BLK, BLK), BLK)
        left, right = sides()

        def shares(query, key, mask):
            scores = product_t(query, key).reshape(group, HALF, BLK) + mask[None]
            top = jnp.max(scores, axis=-1, keepdims=True)
            weights = jnp.exp2((scores - top) * FACTOR)
            return weights / jnp.sum(weights, axis=-1, keepdims=True)

        for at in range(taken):
            key = kbuf[own_rows, at * HEAD : (at + 1) * HEAD]
            query = corner_q[:, at * width : (at + 1) * width]
            low = shares(stacked(query[HALF:]), key, low_bias)
            high = shares(stacked(flipped(query[:HALF])), flipped(key), high_bias)
            mixed = jnp.where(right[None], high, first.astype(jnp.float32))
            mixed = jnp.where(left[None], low, mixed).astype(jnp.bfloat16)
            value = vbuf[own_rows, at * HEAD : (at + 1) * HEAD]
            for g in range(group):
                place = slice(at * width + g * HEAD, at * width + (g + 1) * HEAD)
                corner_out[:HALF, place] = mixed[g]
                corner_out[HALF:, place] = value[g * 16 : (g + 1) * 16]
        corner_stores = []
        for at in range(taken):
            rows_to = pl.ds(len(items) * BLK + at * CORNER, CORNER)
            corner_stores.append(start(corner_out.at[:, pl.ds(at * width, width)], outs[0].at[rows_to]))

    def block_of(place):
        at = jnp.int32(items[-1])
        for other in range(len(items) - 1):
            at = jnp.where(place == other, jnp.int32(items[other]), at)
        return at + (first <= at).astype(jnp.int32)

    def build_bias(block):
        for back in range(TREE_MOST):
            at = (TREE_MOST - 1 - back) * BLK
            bias[:, at : at + BLK] = jnp.where(related(block, back), 0.0, NEG)

    def mixture(query, key, value):
        scores = product_t(stacked(query), key)
        scores = scores.reshape(group, BLK, SPAN) + bias[...][None]
        top = jnp.max(scores, axis=-1, keepdims=True)
        weights = jnp.exp2((scores - top) * FACTOR)
        totals = jnp.sum(weights, axis=-1, keepdims=True)
        rounded = weights.astype(jnp.bfloat16).reshape(group * BLK, SPAN)
        mixed = product(rounded, value)
        mixed = (mixed.reshape(group, BLK, HEAD) / totals).astype(jnp.bfloat16)
        return jnp.concatenate([mixed[g] for g in range(group)], axis=1)

    if last:
        rows_ready()
        build_bias(TREE_MOST)
        for copy in kv_copies:
            copy.wait()
        stores = []
        window = slice(TREE_MOST * BLK, TREE_MOST * BLK + SPAN)
        for at, copy in enumerate(query_copies):
            lanes = slice(at * HEAD, (at + 1) * HEAD)
            place = slice(at * width, (at + 1) * width)
            copy.wait()
            last_out[:, place] = mixture(last_q[:, place], kbuf[window, lanes], vbuf[window, lanes])
            stores.append(start(last_out.at[:, place], outs[0].at[:, place]))
        for copy in stores:
            copy.wait()
        return

    def body(skipped, taken, query_ref, out_ref):
        step = marks[count]
        marks[count] = step + 1
        block, head = (block_of(lax.div(step, taken)), lax.rem(step, taken))

        if not corner:
            pl.when(step == 0)(all_ready)

        pl.when(head == 0)(lambda: build_bias(block))
        window = pl.ds(pl.multiple_of(block * BLK, BLK), SPAN)
        at = pl.ds(pl.multiple_of((skipped + head) * HEAD, HEAD), HEAD)
        out_ref[...] = mixture(query_ref[0], kbuf[window, at], vbuf[window, at])

    for out, heads_here in zip(outs, groups):
        if not items:
            continue
        marks[count] = 0
        pltpu.emit_pipeline(
            functools.partial(body, heads_here[0] - heads[0], len(heads_here)),
            grid=(len(items), len(heads_here)),
            in_specs=[pl.BlockSpec((1, BLK, width), lambda i, h, at=heads_here[0]: (path, block_of(i), at + h))],
            out_specs=[pl.BlockSpec((BLK, width), lambda i, h: (i, h))],
        )(queries, out.at[pl.ds(0, len(items) * BLK)])
    if corner:
        for copy in corner_stores:
            copy.wait()
    if pack:
        for copy in pack_stores:
            copy.wait()


def attend(payload, groups, items, operands, after=(), halo=None, corner=False, pack=False, last=False, weight=0):
    lengths, queries, keys, values, seg, par = operands
    rows, columns = queries.shape[1:]
    width = columns // (keys.shape[2] // HEAD)
    count = rows // BLK
    heads = [head for group in groups for head in group]
    sizes = [(len(items) * BLK, len(group) * width) for group in groups]
    if corner:
        sizes[0] = (len(items) * BLK + len(heads) * CORNER, width)
    out_shape = [jax.ShapeDtypeStruct(size, jnp.bfloat16) for size in sizes]
    scratch = [
        pltpu.VMEM((REACH + rows, len(heads) * HEAD), jnp.bfloat16),
        pltpu.VMEM((REACH + rows, len(heads) * HEAD), jnp.bfloat16),
        pltpu.VMEM((BLK, SPAN), jnp.float32),
        pltpu.VMEM(seg.shape, jnp.int32),
        pltpu.VMEM(par.shape, jnp.int32),
        pltpu.VMEM((1, REACH + rows), jnp.int32),
        pltpu.VMEM((1, REACH + rows), jnp.int32),
        pltpu.SMEM(lengths.shape, jnp.int32),
        pltpu.SMEM((count + 1,), jnp.int32),
        pltpu.SemaphoreType.DMA((16,)),
    ]
    if halo is not None:
        scratch.append(pltpu.VMEM((INFO, keys.shape[2]), jnp.bfloat16))
    if corner:
        scratch.append(pltpu.VMEM((BLK, len(heads) * width), jnp.bfloat16))
        scratch.append(pltpu.VMEM((CORNER, len(heads) * width), jnp.bfloat16))
    if pack:
        packed = (2, 2, REACH + INFO, keys.shape[2])
        out_shape += [jax.ShapeDtypeStruct(packed[1:], jnp.bfloat16)] * 2
        scratch.append(pltpu.VMEM(packed, jnp.bfloat16))
    if last:
        scratch += [pltpu.VMEM((BLK, len(heads) * width), jnp.bfloat16)] * 2
    inputs = [lengths, queries, keys, values, seg, par] + ([] if halo is None else [halo])

    def kernel(*refs):
        refs = refs[: len(inputs)] + refs[len(inputs) + len(after) :]
        attend_kernel(payload, groups, items, corner, pack, halo is not None, last, *refs)

    return pl.pallas_call(
        kernel,
        out_shape=out_shape,
        in_specs=[HBM] * 6 + [ANY] * (len(inputs) - 6 + len(after)),
        out_specs=[ANY] * len(out_shape),
        scratch_shapes=scratch,
        compiler_params=pltpu.CompilerParams(vmem_limit_bytes=VMEM_LIMIT),
        cost_estimate=cost(weight),
    )(*inputs, *after)


def behind(value, *after):
    return pl.pallas_call(
        lambda *refs: None,
        out_shape=jax.ShapeDtypeStruct(value.shape, value.dtype),
        in_specs=[ANY] * (1 + len(after)),
        out_specs=ANY,
        input_output_aliases={0: 0},
        cost_estimate=cost(0),
    )(value, *after)


def place_kernel(pieces, aliased, *refs):
    refs = list(refs)
    sources = [[refs.pop(0)] if piece[1] else [refs.pop(0), refs.pop(0)] for piece in pieces]
    refs = refs[aliased:]
    forward, back = refs[:2]
    stages = refs[2 : 2 + len(pieces)]
    refs = refs[2 + len(pieces) :]
    blocks = {at: refs.pop(0) for at, piece in enumerate(pieces) if piece[0] == "corner"}
    in_sems, out_sems = refs
    width = forward.shape[1] // KV_HEADS
    group = width // HEAD
    where = lax.axis_index("pipe")
    even = lax.rem(where, 2) == 0
    edge = (where == 0) | (where == lax.axis_size("pipe") - 1)

    parts = []
    for at, (kind, _, _, items, top) in enumerate(pieces):
        if kind == "plain":
            parts += [(at, item * BLK, BLK, 0) for item in range(len(items))]
        else:
            parts.append((at, 0, stages[at].shape[0], top))

    def load(part, source):
        at, top, height, below = parts[part]
        view = (pl.ds(below + top, height), pl.ds(0, stages[at].shape[1]))
        return pltpu.make_async_copy(source.at[view], stages[at].at[pl.ds(top, height)], in_sems.at[part])

    for part, (at, _, _, _) in enumerate(parts):
        if len(sources[at]) == 1:
            load(part, sources[at][0]).start()
        else:
            pl.when(edge)(lambda: load(part, sources[at][1]).start())
            pl.when(jnp.logical_not(edge))(lambda: load(part, sources[at][0]).start())

    first = {}
    stores = []

    def store(at, source, block):
        _, swap, heads, _, _ = pieces[at]
        columns = pl.ds(heads[0] * width, len(heads) * width)
        rows = pl.ds(pl.multiple_of(block * BLK, BLK), BLK)
        for to_forward, target in ((even != swap, forward), (even == swap, back)):

            @pl.when(to_forward)
            def _():
                pltpu.make_async_copy(source, target.at[rows, columns], out_sems.at[len(stores)]).start()

        stores.append(pltpu.make_async_copy(source, forward.at[rows, columns], out_sems.at[len(stores)]))

    for part, (at, top, _, _) in enumerate(parts):
        kind, swap, heads, items, _ = pieces[at]
        load(part, sources[at][0]).wait()
        if kind == "plain":
            store(at, stages[at].at[pl.ds(top, BLK)], plain_block(first[swap], items[top // BLK]))
        elif swap not in first:
            tile = stages[at][:16, :HEAD].astype(jnp.float32)
            row = lax.broadcasted_iota(jnp.int32, tile.shape, 0)
            lane = lax.broadcasted_iota(jnp.int32, tile.shape, 1)
            first[swap] = jnp.sum(jnp.where((row == 0) & (lane == HALF), tile, 0.0)).astype(jnp.int32)

    left, right = sides()
    for at, decoded in blocks.items():
        value = stacked(stages[at][HALF:])
        turned = flipped(value)
        shares = stacked(stages[at][:HALF].astype(jnp.float32)).reshape(group, HALF, BLK)

        def context(side, basis):
            kept = jnp.where(side[None], shares, 0.0)
            rest = 1.0 - jnp.sum(kept, axis=-1, keepdims=True)
            mixed = product(kept.astype(jnp.bfloat16).reshape(group * HALF, BLK), basis)
            mixed = mixed.reshape(group, HALF, HEAD) + rest * basis[HALF:].astype(jnp.float32)[None]
            mixed = mixed.astype(jnp.bfloat16)
            return jnp.concatenate([mixed[g] for g in range(group)], axis=1)

        decoded[HALF:] = context(left, value)
        decoded[:HALF] = flipped(context(right, turned))
        store(at, decoded, first[pieces[at][1]])
    for copy in stores:
        copy.wait()


def place(pieces, rows, outs=(), weight=0):
    arrays = [array for piece in pieces for array in piece[1]]
    columns = next(piece[1][0].shape[1] // len(piece[3]) for piece in pieces if piece[3]) * KV_HEADS
    shape = jax.ShapeDtypeStruct((rows, columns), jnp.bfloat16)
    width = columns // KV_HEADS
    corners = {"guide": (16, HEAD), "corner": (CORNER, width)}
    held = [corners.get(kind, (len(items) * BLK, len(heads) * width)) for kind, _, _, heads, items, _ in pieces]
    decoded = [(BLK, width) for piece in pieces if piece[0] == "corner"]
    return pl.pallas_call(
        functools.partial(place_kernel, [(piece[0],) + piece[2:] for piece in pieces], len(outs)),
        out_shape=[shape, shape],
        in_specs=[ANY] * len(arrays) + [HBM] * len(outs),
        out_specs=[HBM, HBM],
        scratch_shapes=[pltpu.VMEM(size, jnp.bfloat16) for size in held + decoded]
        + [pltpu.SemaphoreType.DMA((4 * len(pieces),))] * 2,
        input_output_aliases={len(arrays) + i: i for i in range(len(outs))},
        compiler_params=pltpu.CompilerParams(vmem_limit_bytes=24 * 1024 * 1024),
        cost_estimate=cost(weight),
    )(*arrays, *outs)


def cost(weight):
    return pl.CostEstimate(flops=1024 + weight * 1000000, bytes_accessed=1024, transcendentals=0)


PLACE_WEIGHT = 0
DIRECT_WEIGHT = 100000

SWAP = [(0, 1), (1, 0), (2, 3), (3, 2)]
DIAGONAL = [(1, 2), (2, 1)]
ACROSS = [(1, 3), (2, 0)]
ONWARD = [(3, 2), (0, 1)]


def on_device(queries, keys, values, segment, parent, tree_lengths):
    rows = queries.shape[2]
    operands = (tree_lengths[0], queries[0], keys[0], values[0], segment[0], parent[0])
    ring = [(source, source + 1) for source in range(lax.axis_size("dp") - 1)]
    every = tuple(range(KV_HEADS))

    (swap_0,) = attend(0, ((0, 1),), (2,), operands, last=True)
    got_0 = lax.ppermute(swap_0, "pipe", SWAP)
    corner, halo, far_halo = attend(0, (every,), (), operands, after=(swap_0,), corner=True, pack=True)
    got_corner = lax.ppermute(corner, "pipe", SWAP)
    halo = lax.ppermute(halo, "dp", ring)
    far_halo = lax.ppermute(far_halo, "dp", ring)
    (swap_1,) = attend(0, ((2, 3),), (2,), operands, after=(corner, got_0), last=True)
    got_1 = lax.ppermute(swap_1, "pipe", SWAP)
    (swap_2,) = attend(0, (every,), (0, 1), operands, after=(swap_1,), halo=halo)
    got_2 = lax.ppermute(swap_2, "pipe", SWAP)
    routed_1, routed_2 = attend(1, ((0,), (1,)), (0, 1, 2), operands, after=(swap_2,), halo=far_halo, corner=True)
    across_1 = lax.ppermute(routed_1, "pipe", ACROSS)
    direct_1, direct_2 = attend(
        1,
        ((2,), (3,)),
        (0, 1, 2),
        operands,
        after=(routed_1, got_1, got_corner),
        halo=far_halo,
        corner=True,
        weight=DIRECT_WEIGHT,
    )
    diagonal_1 = lax.ppermute(direct_1, "pipe", DIAGONAL)
    across_2 = lax.ppermute(behind(routed_2, direct_1), "pipe", ACROSS)
    diagonal_2 = lax.ppermute(behind(direct_2, across_2), "pipe", DIAGONAL)
    onward_1 = lax.ppermute(behind(across_1, direct_1), "pipe", ONWARD)
    onward_2 = lax.ppermute(behind(across_2, direct_1), "pipe", ONWARD)
    outs = place(
        [("corner", (got_corner,), True, (head,), (), head * CORNER) for head in every]
        + [
            ("plain", (got_0,), True, (0, 1), (2,), 0),
            ("plain", (got_1,), True, (2, 3), (2,), 0),
            ("plain", (got_2,), True, every, (0, 1), 0),
        ],
        rows,
        weight=PLACE_WEIGHT,
    )
    below = TREE_MOST * BLK
    onward_1, diagonal_1 = ((onward_1, routed_1), (diagonal_1, direct_1))
    outs = place(
        [
            ("corner", onward_1, False, (0,), (), below),
            ("corner", onward_1, False, (1,), (), below + CORNER),
            ("corner", diagonal_1, False, (2,), (), below),
            ("corner", diagonal_1, False, (3,), (), below + CORNER),
            ("plain", onward_1, False, (0,), (0, 1, 2), 0),
            ("plain", diagonal_1, False, (2,), (0, 1, 2), 0),
        ],
        rows,
        outs,
    )
    forward, back = place(
        [
            ("guide", diagonal_1, False, (), (), below),
            ("plain", (onward_2, routed_2), False, (1,), (0, 1, 2), 0),
            ("plain", (diagonal_2, direct_2), False, (3,), (0, 1, 2), 0),
        ],
        rows,
        outs,
    )
    return (forward[None], back[None])


def solution(mesh):
    return jax.shard_map(
        on_device,
        mesh=mesh,
        in_specs=(
            P("pipe", None, "dp", None),
            P("pipe", None, "dp", None),
            P("pipe", None, "dp", None),
            P("pipe", None, "dp"),
            P("pipe", None, "dp"),
            P("pipe", None, None),
        ),
        out_specs=(P("pipe", "dp", None), P("pipe", "dp", None)),
        check_vma=False,
    )
```

```python
import functools
import math

import jax
import jax.numpy as jnp
from jax import lax
from jax.experimental import pallas as pl
from jax.experimental.pallas import tpu as pltpu
from jax.sharding import PartitionSpec as P

BLK = 128
TREE_MOST = 3
KV_HEADS = 4
HEAD = 128
REACH = (TREE_MOST - 1) * BLK
SPAN = TREE_MOST * BLK
NEG = -1e30
FACTOR = math.log2(math.e) / math.sqrt(HEAD)

HALF = BLK // 2
CORNER = HALF + 16
INFO = 16
VMEM_LIMIT = 60 * 1024 * 1024

ANY = pl.BlockSpec(memory_space=pl.ANY)
HBM = pl.BlockSpec(memory_space=pltpu.HBM)


def flipped(array):
    count = array.shape[0]
    rows = lax.broadcasted_iota(jnp.int32, (count, count), 0)
    lanes = lax.broadcasted_iota(jnp.int32, (count, count), 1)
    swap = (rows + lanes == count - 1).astype(jnp.bfloat16)
    return jnp.dot(swap, array, preferred_element_type=jnp.float32).astype(jnp.bfloat16)


def stacked(array):
    return jnp.concatenate([array[:, at : at + HEAD] for at in range(0, array.shape[1], HEAD)], axis=0)


def product(left, right):
    return jnp.dot(left, right, preferred_element_type=jnp.float32)


def product_t(left, right):
    return lax.dot_general(left, right, (((1,), (1,)), ((), ())), preferred_element_type=jnp.float32)


def sides():
    lane = lax.broadcasted_iota(jnp.int32, (HALF, BLK), 1)
    gap = lax.broadcasted_iota(jnp.int32, (HALF, BLK), 0) + HALF
    return (lane < gap, lane > gap)


def plain_block(first, at):
    return at + (first <= at).astype(jnp.int32)


def attend_kernel(payload, groups, items, corner, pack, halo, last, *refs):
    heads = [head for group in groups for head in group]
    refs = list(refs)
    lengths_in, queries, keys, values, seg_in, par_in = refs[:6]
    refs = refs[6:]
    halo_in = refs.pop(0) if halo else None
    outs = [refs.pop(0) for _ in groups]
    pack_outs = [refs.pop(0), refs.pop(0)] if pack else None
    kbuf, vbuf, bias, segs, pars, seg, par, lengths, marks, sems = refs[:10]
    refs = refs[10:]
    if halo:
        info = refs.pop(0)
    if corner:
        corner_q, corner_out = refs[:2]
        refs = refs[2:]
    if pack:
        packed = refs.pop(0)
    if last:
        last_q, last_out = refs[:2]
    rows = keys.shape[1]
    kv_heads = keys.shape[2] // HEAD
    width = queries.shape[2] // kv_heads
    group = width // HEAD
    count = rows // BLK
    taken = len(heads)
    path = lax.rem(lax.axis_index("pipe"), 2)
    path = path if payload == 0 else 1 - path
    first_block = lax.axis_index("dp") * count
    lanes = pl.ds(heads[0] * HEAD, taken * HEAD)

    started = []

    def start(source, target):
        copy = pltpu.make_async_copy(source, target, sems.at[len(started)])
        copy.start()
        started.append(copy)
        return copy

    lengths_copy = start(lengths_in, lengths)
    row_copies = [start(seg_in, segs), start(par_in, pars)]
    query_copies = []
    if last:
        for at, head in enumerate(heads):
            source = queries.at[path, pl.ds(TREE_MOST * BLK, BLK), pl.ds(head * width, width)]
            query_copies.append(start(source, last_q.at[:, pl.ds(at * width, width)]))
    kv_copies = []
    for which, (source, target) in enumerate(((keys, kbuf), (values, vbuf))):
        kv_copies.append(start(source.at[path, :, lanes], target.at[pl.ds(REACH, rows)]))
        if halo:
            kv_copies.append(start(halo_in.at[which, pl.ds(0, REACH), lanes], target.at[pl.ds(0, REACH)]))
    if halo:
        row_copies.append(start(halo_in.at[0, pl.ds(REACH, INFO)], info))
    pack_copies = []
    if pack:
        for each in range(2):
            for which, source in enumerate((keys, values)):
                source = source.at[each, pl.ds(rows - REACH, REACH)]
                pack_copies.append(start(source, packed.at[each, which, pl.ds(0, REACH)]))

    lengths_copy.wait()

    def step(entry, carry):
        end, begins = carry
        end = end + lengths[path, entry]
        return (end, tuple(jnp.where(end <= first_block + at, end, begin) for at, begin in enumerate(begins)))

    zero = jnp.int32(0)
    _, begins = lax.fori_loop(0, lengths.shape[1], step, (zero, (zero,) * count), unroll=8)
    first = jnp.int32(TREE_MOST - 1)
    for at in reversed(range(count)):
        marks[at] = begins[at]
        if at < TREE_MOST - 1:
            first = jnp.where(begins[at] == first_block + at, at, first)
    if corner:
        columns = pl.ds(heads[0] * width, taken * width)
        query_copy = start(queries.at[path, pl.ds(pl.multiple_of(first * BLK, BLK), BLK), columns], corner_q)

    def rows_ready():
        for copy in row_copies:
            copy.wait()
        for source, target in ((segs, seg), (pars, par)):
            target[:, REACH:] = jnp.where(path == 0, source[0:1], source[1:2])
        if halo:
            numbers = info[...].astype(jnp.float32)
            seg[:, :REACH] = (numbers[0:1, :REACH] * 128.0 + numbers[1:2, :REACH]).astype(jnp.int32)
            par[:, :REACH] = (numbers[2:3, :REACH] * 128.0 + numbers[3:4, :REACH]).astype(jnp.int32)

    def all_ready():
        rows_ready()
        for copy in kv_copies:
            copy.wait()

    if corner:
        all_ready()
    pack_stores = []

    def store_pack():
        for each in range(2):
            at = lax.broadcasted_iota(jnp.int32, (INFO, REACH), 0)
            numbers = jnp.zeros((INFO, REACH), jnp.int32)
            for which, source in enumerate((segs, pars)):
                row = source[each : each + 1, rows - REACH :]
                numbers = jnp.where(at == 2 * which, row >> 7, numbers)
                numbers = jnp.where(at == 2 * which + 1, row & 127, numbers)
            numbers = numbers.astype(jnp.float32).astype(jnp.bfloat16)
            packed[each, 0, REACH:, :REACH] = numbers
            packed[each, 0, REACH:, REACH:] = jnp.zeros((INFO, keys.shape[2] - REACH), jnp.bfloat16)
            packed[each, 1, REACH:, :] = jnp.zeros((INFO, keys.shape[2]), jnp.bfloat16)
        for copy in pack_copies:
            copy.wait()
        pack_stores.append(start(packed.at[path], pack_outs[0]))
        pack_stores.append(start(packed.at[1 - path], pack_outs[1]))

    if pack and not last:
        store_pack()

    def column(row):
        return jnp.transpose(jnp.broadcast_to(row, (BLK, BLK)))

    def related(block, back):
        ours = pl.ds(pl.multiple_of(REACH + block * BLK, BLK), BLK)
        theirs = pl.ds(pl.multiple_of(REACH + (block - back) * BLK, BLK), BLK)
        key_seg = seg[:, theirs]
        query_seg, query_par = (column(seg[:, ours]), column(par[:, ours]))
        found = (key_seg == query_seg) | (key_seg == query_par) | (par[:, theirs] == key_seg)
        if back:
            return found & (first_block + block - back >= marks[block])
        lane = lax.broadcasted_iota(jnp.int32, (BLK, BLK), 1)
        return found & (lane <= lax.broadcasted_iota(jnp.int32, (BLK, BLK), 0))

    if corner:
        query_copy.wait()
        seen = related(first, 0).astype(jnp.float32).astype(jnp.bfloat16)
        turned = jnp.transpose(flipped(jnp.transpose(flipped(seen[:HALF]).astype(jnp.float32)).astype(jnp.bfloat16)).astype(jnp.float32))
        low_bias = jnp.where(seen[HALF:].astype(jnp.float32) > 0.5, 0.0, NEG)
        high_bias = jnp.where(turned > 0.5, 0.0, NEG)
        own_rows = pl.ds(pl.multiple_of(REACH + first * BLK, BLK), BLK)
        left, right = sides()

        def shares(query, key, mask):
            scores = product_t(query, key).reshape(group, HALF, BLK) + mask[None]
            top = jnp.max(scores, axis=-1, keepdims=True)
            weights = jnp.exp2((scores - top) * FACTOR)
            return weights / jnp.sum(weights, axis=-1, keepdims=True)

        for at in range(taken):
            key = kbuf[own_rows, at * HEAD : (at + 1) * HEAD]
            query = corner_q[:, at * width : (at + 1) * width]
            low = shares(stacked(query[HALF:]), key, low_bias)
            high = shares(stacked(flipped(query[:HALF])), flipped(key), high_bias)
            mixed = jnp.where(right[None], high, first.astype(jnp.float32))
            mixed = jnp.where(left[None], low, mixed).astype(jnp.bfloat16)
            value = vbuf[own_rows, at * HEAD : (at + 1) * HEAD]
            for g in range(group):
                place = slice(at * width + g * HEAD, at * width + (g + 1) * HEAD)
                corner_out[:HALF, place] = mixed[g]
                corner_out[HALF:, place] = value[g * 16 : (g + 1) * 16]
        corner_stores = []
        for at in range(taken):
            rows_to = pl.ds(len(items) * BLK + at * CORNER, CORNER)
            corner_stores.append(start(corner_out.at[:, pl.ds(at * width, width)], outs[0].at[rows_to]))

    def block_of(place):
        at = jnp.int32(items[-1])
        for other in range(len(items) - 1):
            at = jnp.where(place == other, jnp.int32(items[other]), at)
        return at + (first <= at).astype(jnp.int32)

    def build_bias(block):
        for back in range(TREE_MOST):
            at = (TREE_MOST - 1 - back) * BLK
            bias[:, at : at + BLK] = jnp.where(related(block, back), 0.0, NEG)

    def mixture(query, key, value):
        scores = product_t(stacked(query), key)
        scores = scores.reshape(group, BLK, SPAN) + bias[...][None]
        top = jnp.max(scores, axis=-1, keepdims=True)
        weights = jnp.exp2((scores - top) * FACTOR)
        totals = jnp.sum(weights, axis=-1, keepdims=True)
        rounded = weights.astype(jnp.bfloat16).reshape(group * BLK, SPAN)
        mixed = product(rounded, value)
        mixed = (mixed.reshape(group, BLK, HEAD) / totals).astype(jnp.bfloat16)
        return jnp.concatenate([mixed[g] for g in range(group)], axis=1)

    if last:
        rows_ready()
        build_bias(TREE_MOST)
        for copy in kv_copies:
            copy.wait()
        stores = []
        window = slice(TREE_MOST * BLK, TREE_MOST * BLK + SPAN)
        for at, copy in enumerate(query_copies):
            lanes = slice(at * HEAD, (at + 1) * HEAD)
            place = slice(at * width, (at + 1) * width)
            copy.wait()
            last_out[:, place] = mixture(last_q[:, place], kbuf[window, lanes], vbuf[window, lanes])
            stores.append(start(last_out.at[:, place], outs[0].at[:, place]))
            if pack and at == 0:
                store_pack()
        for copy in stores + pack_stores:
            copy.wait()
        return

    def body(skipped, taken, query_ref, out_ref):
        step = marks[count]
        marks[count] = step + 1
        block, head = (block_of(lax.div(step, taken)), lax.rem(step, taken))

        if not corner:
            pl.when(step == 0)(all_ready)

        pl.when(head == 0)(lambda: build_bias(block))
        window = pl.ds(pl.multiple_of(block * BLK, BLK), SPAN)
        at = pl.ds(pl.multiple_of((skipped + head) * HEAD, HEAD), HEAD)
        out_ref[...] = mixture(query_ref[0], kbuf[window, at], vbuf[window, at])

    for out, heads_here in zip(outs, groups):
        if not items:
            continue
        marks[count] = 0
        pltpu.emit_pipeline(
            functools.partial(body, heads_here[0] - heads[0], len(heads_here)),
            grid=(len(items), len(heads_here)),
            in_specs=[pl.BlockSpec((1, BLK, width), lambda i, h, at=heads_here[0]: (path, block_of(i), at + h))],
            out_specs=[pl.BlockSpec((BLK, width), lambda i, h: (i, h))],
        )(queries, out.at[pl.ds(0, len(items) * BLK)])
    if corner:
        for copy in corner_stores:
            copy.wait()
    for copy in pack_stores:
        copy.wait()


def attend(payload, groups, items, operands, after=(), halo=None, corner=False, pack=False, last=False, weight=0):
    lengths, queries, keys, values, seg, par = operands
    rows, columns = queries.shape[1:]
    width = columns // (keys.shape[2] // HEAD)
    count = rows // BLK
    heads = [head for group in groups for head in group]
    sizes = [(len(items) * BLK, len(group) * width) for group in groups]
    if corner:
        sizes[0] = (len(items) * BLK + len(heads) * CORNER, width)
    out_shape = [jax.ShapeDtypeStruct(size, jnp.bfloat16) for size in sizes]
    scratch = [
        pltpu.VMEM((REACH + rows, len(heads) * HEAD), jnp.bfloat16),
        pltpu.VMEM((REACH + rows, len(heads) * HEAD), jnp.bfloat16),
        pltpu.VMEM((BLK, SPAN), jnp.float32),
        pltpu.VMEM(seg.shape, jnp.int32),
        pltpu.VMEM(par.shape, jnp.int32),
        pltpu.VMEM((1, REACH + rows), jnp.int32),
        pltpu.VMEM((1, REACH + rows), jnp.int32),
        pltpu.SMEM(lengths.shape, jnp.int32),
        pltpu.SMEM((count + 1,), jnp.int32),
        pltpu.SemaphoreType.DMA((20,)),
    ]
    if halo is not None:
        scratch.append(pltpu.VMEM((INFO, keys.shape[2]), jnp.bfloat16))
    if corner:
        scratch.append(pltpu.VMEM((BLK, len(heads) * width), jnp.bfloat16))
        scratch.append(pltpu.VMEM((CORNER, len(heads) * width), jnp.bfloat16))
    if pack:
        packed = (2, 2, REACH + INFO, keys.shape[2])
        out_shape += [jax.ShapeDtypeStruct(packed[1:], jnp.bfloat16)] * 2
        scratch.append(pltpu.VMEM(packed, jnp.bfloat16))
    if last:
        scratch += [pltpu.VMEM((BLK, len(heads) * width), jnp.bfloat16)] * 2
    inputs = [lengths, queries, keys, values, seg, par] + ([] if halo is None else [halo])

    def kernel(*refs):
        refs = refs[: len(inputs)] + refs[len(inputs) + len(after) :]
        attend_kernel(payload, groups, items, corner, pack, halo is not None, last, *refs)

    return pl.pallas_call(
        kernel,
        out_shape=out_shape,
        in_specs=[HBM] * 6 + [ANY] * (len(inputs) - 6 + len(after)),
        out_specs=[ANY] * len(out_shape),
        scratch_shapes=scratch,
        compiler_params=pltpu.CompilerParams(vmem_limit_bytes=VMEM_LIMIT),
        cost_estimate=cost(weight),
    )(*inputs, *after)


def behind(value, *after):
    return pl.pallas_call(
        lambda *refs: None,
        out_shape=jax.ShapeDtypeStruct(value.shape, value.dtype),
        in_specs=[ANY] * (1 + len(after)),
        out_specs=ANY,
        input_output_aliases={0: 0},
        cost_estimate=cost(0),
    )(value, *after)


def place_kernel(pieces, aliased, *refs):
    refs = list(refs)
    sources = [[refs.pop(0)] if piece[1] else [refs.pop(0), refs.pop(0)] for piece in pieces]
    refs = refs[aliased:]
    forward, back = refs[:2]
    stages = refs[2 : 2 + len(pieces)]
    refs = refs[2 + len(pieces) :]
    blocks = {at: refs.pop(0) for at, piece in enumerate(pieces) if piece[0] == "corner"}
    in_sems, out_sems = refs
    width = forward.shape[1] // KV_HEADS
    group = width // HEAD
    where = lax.axis_index("pipe")
    even = lax.rem(where, 2) == 0
    edge = (where == 0) | (where == lax.axis_size("pipe") - 1)

    parts = []
    for at, (kind, _, _, items, top) in enumerate(pieces):
        if kind == "plain":
            parts += [(at, item * BLK, BLK, 0) for item in range(len(items))]
        else:
            parts.append((at, 0, stages[at].shape[0], top))

    def load(part, source):
        at, top, height, below = parts[part]
        view = (pl.ds(below + top, height), pl.ds(0, stages[at].shape[1]))
        return pltpu.make_async_copy(source.at[view], stages[at].at[pl.ds(top, height)], in_sems.at[part])

    for part, (at, _, _, _) in enumerate(parts):
        if len(sources[at]) == 1:
            load(part, sources[at][0]).start()
        else:
            pl.when(edge)(lambda: load(part, sources[at][1]).start())
            pl.when(jnp.logical_not(edge))(lambda: load(part, sources[at][0]).start())

    first = {}
    stores = []

    def store(at, source, block):
        _, swap, heads, _, _ = pieces[at]
        columns = pl.ds(heads[0] * width, len(heads) * width)
        rows = pl.ds(pl.multiple_of(block * BLK, BLK), BLK)
        for to_forward, target in ((even != swap, forward), (even == swap, back)):

            @pl.when(to_forward)
            def _():
                pltpu.make_async_copy(source, target.at[rows, columns], out_sems.at[len(stores)]).start()

        stores.append(pltpu.make_async_copy(source, forward.at[rows, columns], out_sems.at[len(stores)]))

    for part, (at, top, _, _) in enumerate(parts):
        kind, swap, heads, items, _ = pieces[at]
        load(part, sources[at][0]).wait()
        if kind == "plain":
            store(at, stages[at].at[pl.ds(top, BLK)], plain_block(first[swap], items[top // BLK]))
        elif swap not in first:
            tile = stages[at][:16, :HEAD].astype(jnp.float32)
            row = lax.broadcasted_iota(jnp.int32, tile.shape, 0)
            lane = lax.broadcasted_iota(jnp.int32, tile.shape, 1)
            first[swap] = jnp.sum(jnp.where((row == 0) & (lane == HALF), tile, 0.0)).astype(jnp.int32)

    left, right = sides()
    for at, decoded in blocks.items():
        value = stacked(stages[at][HALF:])
        turned = flipped(value)
        shares = stacked(stages[at][:HALF].astype(jnp.float32)).reshape(group, HALF, BLK)

        def context(side, basis):
            kept = jnp.where(side[None], shares, 0.0)
            rest = 1.0 - jnp.sum(kept, axis=-1, keepdims=True)
            mixed = product(kept.astype(jnp.bfloat16).reshape(group * HALF, BLK), basis)
            mixed = mixed.reshape(group, HALF, HEAD) + rest * basis[HALF:].astype(jnp.float32)[None]
            mixed = mixed.astype(jnp.bfloat16)
            return jnp.concatenate([mixed[g] for g in range(group)], axis=1)

        decoded[HALF:] = context(left, value)
        decoded[:HALF] = flipped(context(right, turned))
        store(at, decoded, first[pieces[at][1]])
    for copy in stores:
        copy.wait()


def place(pieces, rows, outs=(), weight=0):
    arrays = [array for piece in pieces for array in piece[1]]
    columns = next(piece[1][0].shape[1] // len(piece[3]) for piece in pieces if piece[3]) * KV_HEADS
    shape = jax.ShapeDtypeStruct((rows, columns), jnp.bfloat16)
    width = columns // KV_HEADS
    corners = {"guide": (16, HEAD), "corner": (CORNER, width)}
    held = [corners.get(kind, (len(items) * BLK, len(heads) * width)) for kind, _, _, heads, items, _ in pieces]
    decoded = [(BLK, width) for piece in pieces if piece[0] == "corner"]
    return pl.pallas_call(
        functools.partial(place_kernel, [(piece[0],) + piece[2:] for piece in pieces], len(outs)),
        out_shape=[shape, shape],
        in_specs=[ANY] * len(arrays) + [HBM] * len(outs),
        out_specs=[HBM, HBM],
        scratch_shapes=[pltpu.VMEM(size, jnp.bfloat16) for size in held + decoded]
        + [pltpu.SemaphoreType.DMA((4 * len(pieces),))] * 2,
        input_output_aliases={len(arrays) + i: i for i in range(len(outs))},
        compiler_params=pltpu.CompilerParams(vmem_limit_bytes=24 * 1024 * 1024),
        cost_estimate=cost(weight),
    )(*arrays, *outs)


def cost(weight):
    return pl.CostEstimate(flops=1024 + weight * 1000000, bytes_accessed=1024, transcendentals=0)


PLACE_WEIGHT = 0
SWAP_WEIGHT = 2000
DIRECT_WEIGHT = 100000

SWAP = [(0, 1), (1, 0), (2, 3), (3, 2)]
DIAGONAL = [(1, 2), (2, 1)]
ACROSS = [(1, 3), (2, 0)]
ONWARD = [(3, 2), (0, 1)]


def on_device(queries, keys, values, segment, parent, tree_lengths):
    rows = queries.shape[2]
    operands = (tree_lengths[0], queries[0], keys[0], values[0], segment[0], parent[0])
    ring = [(source, source + 1) for source in range(lax.axis_size("dp") - 1)]
    every = tuple(range(KV_HEADS))

    (swap_0,) = attend(0, ((0,),), (2,), operands, last=True)
    got_0 = lax.ppermute(swap_0, "pipe", SWAP)
    swap_1, halo, far_halo = attend(0, ((1, 2, 3),), (2,), operands, after=(swap_0,), pack=True, last=True)
    got_1 = lax.ppermute(swap_1, "pipe", SWAP)
    halo = lax.ppermute(halo, "dp", ring)
    far_halo = lax.ppermute(far_halo, "dp", ring)
    (corner,) = attend(0, (every,), (), operands, after=(swap_1, got_0), corner=True)
    got_corner = lax.ppermute(corner, "pipe", SWAP)
    (swap_2,) = attend(0, (every,), (0, 1), operands, after=(corner,), halo=halo, weight=SWAP_WEIGHT)
    got_2 = lax.ppermute(swap_2, "pipe", SWAP)
    routed_1, routed_2 = attend(1, ((0,), (1,)), (0, 1, 2), operands, after=(swap_2,), halo=far_halo, corner=True)
    across_1 = lax.ppermute(routed_1, "pipe", ACROSS)
    direct_1, direct_2 = attend(
        1,
        ((2,), (3,)),
        (0, 1, 2),
        operands,
        after=(routed_1, got_1, got_corner),
        halo=far_halo,
        corner=True,
        weight=DIRECT_WEIGHT,
    )
    diagonal_1 = lax.ppermute(direct_1, "pipe", DIAGONAL)
    across_2 = lax.ppermute(behind(routed_2, direct_1), "pipe", ACROSS)
    diagonal_2 = lax.ppermute(behind(direct_2, across_2), "pipe", DIAGONAL)
    onward_1 = lax.ppermute(behind(across_1, direct_1), "pipe", ONWARD)
    onward_2 = lax.ppermute(behind(across_2, direct_1), "pipe", ONWARD)
    outs = place(
        [("corner", (got_corner,), True, (head,), (), head * CORNER) for head in every]
        + [
            ("plain", (got_0,), True, (0,), (2,), 0),
            ("plain", (got_1,), True, (1, 2, 3), (2,), 0),
            ("plain", (got_2,), True, every, (0, 1), 0),
        ],
        rows,
        weight=PLACE_WEIGHT,
    )
    below = TREE_MOST * BLK
    onward_1, diagonal_1 = ((onward_1, routed_1), (diagonal_1, direct_1))
    outs = place(
        [
            ("corner", onward_1, False, (0,), (), below),
            ("corner", onward_1, False, (1,), (), below + CORNER),
            ("corner", diagonal_1, False, (2,), (), below),
            ("corner", diagonal_1, False, (3,), (), below + CORNER),
            ("plain", onward_1, False, (0,), (0, 1, 2), 0),
            ("plain", diagonal_1, False, (2,), (0, 1, 2), 0),
        ],
        rows,
        outs,
    )
    forward, back = place(
        [
            ("guide", diagonal_1, False, (), (), below),
            ("plain", (onward_2, routed_2), False, (1,), (0, 1, 2), 0),
            ("plain", (diagonal_2, direct_2), False, (3,), (0, 1, 2), 0),
        ],
        rows,
        outs,
    )
    return (forward[None], back[None])


def solution(mesh):
    return jax.shard_map(
        on_device,
        mesh=mesh,
        in_specs=(
            P("pipe", None, "dp", None),
            P("pipe", None, "dp", None),
            P("pipe", None, "dp", None),
            P("pipe", None, "dp"),
            P("pipe", None, "dp"),
            P("pipe", None, None),
        ),
        out_specs=(P("pipe", "dp", None), P("pipe", "dp", None)),
        check_vma=False,
    )
```

```python
import functools
import math

import jax
import jax.numpy as jnp
from jax import lax
from jax.experimental import pallas as pl
from jax.experimental.pallas import tpu as pltpu
from jax.sharding import PartitionSpec as P

BLK = 128
TREE_MOST = 3
KV_HEADS = 4
HEAD = 128
REACH = (TREE_MOST - 1) * BLK
SPAN = TREE_MOST * BLK
NEG = -1e30
FACTOR = math.log2(math.e) / math.sqrt(HEAD)

HALF = BLK // 2
CORNER = HALF + 16
INFO = 16
RANGE = 80.0
VMEM_LIMIT = 60 * 1024 * 1024

ANY = pl.BlockSpec(memory_space=pl.ANY)
HBM = pl.BlockSpec(memory_space=pltpu.HBM)


def flipped(array):
    count = array.shape[0]
    rows = lax.broadcasted_iota(jnp.int32, (count, count), 0)
    lanes = lax.broadcasted_iota(jnp.int32, (count, count), 1)
    swap = (rows + lanes == count - 1).astype(jnp.bfloat16)
    return jnp.dot(swap, array, preferred_element_type=jnp.float32).astype(jnp.bfloat16)


def stacked(array):
    return jnp.concatenate([array[:, at : at + HEAD] for at in range(0, array.shape[1], HEAD)], axis=0)


def product(left, right):
    return jnp.dot(left, right, preferred_element_type=jnp.float32)


def product_t(left, right):
    return lax.dot_general(left, right, (((1,), (1,)), ((), ())), preferred_element_type=jnp.float32)


def sides():
    lane = lax.broadcasted_iota(jnp.int32, (HALF, BLK), 1)
    gap = lax.broadcasted_iota(jnp.int32, (HALF, BLK), 0) + HALF
    return (lane < gap, lane > gap)


def plain_block(first, at):
    return at + (first <= at).astype(jnp.int32)


def attend_kernel(payload, groups, items, corner, pack, halo, last, *refs):
    heads = [head for group in groups for head in group]
    refs = list(refs)
    lengths_in, queries, keys, values, seg_in, par_in = refs[:6]
    refs = refs[6:]
    halo_in = refs.pop(0) if halo else None
    outs = [refs.pop(0) for _ in groups]
    pack_outs = [refs.pop(0), refs.pop(0)] if pack else None
    kbuf, vbuf, bias, segs, pars, seg, par, lengths, marks, sems = refs[:10]
    refs = refs[10:]
    if halo:
        info = refs.pop(0)
    if corner:
        corner_q, corner_out = refs[:2]
        refs = refs[2:]
    if pack:
        packed = refs.pop(0)
    if last:
        last_q, last_out = refs[:2]
    rows = keys.shape[1]
    kv_heads = keys.shape[2] // HEAD
    width = queries.shape[2] // kv_heads
    group = width // HEAD
    count = rows // BLK
    taken = len(heads)
    path = lax.rem(lax.axis_index("pipe"), 2)
    path = path if payload == 0 else 1 - path
    first_block = lax.axis_index("dp") * count
    lanes = pl.ds(heads[0] * HEAD, taken * HEAD)

    started = []

    def start(source, target):
        copy = pltpu.make_async_copy(source, target, sems.at[len(started)])
        copy.start()
        started.append(copy)
        return copy

    lengths_copy = start(lengths_in, lengths)
    row_copies = [start(seg_in, segs), start(par_in, pars)]
    query_copies = []
    if last:
        for at, head in enumerate(heads):
            source = queries.at[path, pl.ds(TREE_MOST * BLK, BLK), pl.ds(head * width, width)]
            query_copies.append(start(source, last_q.at[:, pl.ds(at * width, width)]))
    kv_copies = []
    for which, (source, target) in enumerate(((keys, kbuf), (values, vbuf))):
        kv_copies.append(start(source.at[path, :, lanes], target.at[pl.ds(REACH, rows)]))
        if halo:
            kv_copies.append(start(halo_in.at[which, pl.ds(0, REACH), lanes], target.at[pl.ds(0, REACH)]))
    if halo:
        row_copies.append(start(halo_in.at[0, pl.ds(REACH, INFO)], info))
    pack_copies = []
    if pack:
        for each in range(2):
            for which, source in enumerate((keys, values)):
                source = source.at[each, pl.ds(rows - REACH, REACH)]
                pack_copies.append(start(source, packed.at[each, which, pl.ds(0, REACH)]))

    lengths_copy.wait()

    def step(entry, carry):
        end, begins = carry
        end = end + lengths[path, entry]
        return (end, tuple(jnp.where(end <= first_block + at, end, begin) for at, begin in enumerate(begins)))

    zero = jnp.int32(0)
    _, begins = lax.fori_loop(0, lengths.shape[1], step, (zero, (zero,) * count), unroll=8)
    first = jnp.int32(TREE_MOST - 1)
    for at in reversed(range(count)):
        marks[at] = begins[at]
        if at < TREE_MOST - 1:
            first = jnp.where(begins[at] == first_block + at, at, first)
    if corner:
        columns = pl.ds(heads[0] * width, taken * width)
        query_copy = start(queries.at[path, pl.ds(pl.multiple_of(first * BLK, BLK), BLK), columns], corner_q)

    def rows_ready():
        for copy in row_copies:
            copy.wait()
        for source, target in ((segs, seg), (pars, par)):
            target[:, REACH:] = jnp.where(path == 0, source[0:1], source[1:2])
        if halo:
            numbers = info[...].astype(jnp.float32)
            seg[:, :REACH] = (numbers[0:1, :REACH] * 128.0 + numbers[1:2, :REACH]).astype(jnp.int32)
            par[:, :REACH] = (numbers[2:3, :REACH] * 128.0 + numbers[3:4, :REACH]).astype(jnp.int32)

    def all_ready():
        rows_ready()
        for copy in kv_copies:
            copy.wait()

    if corner:
        all_ready()
    pack_stores = []

    def store_pack():
        for each in range(2):
            at = lax.broadcasted_iota(jnp.int32, (INFO, REACH), 0)
            numbers = jnp.zeros((INFO, REACH), jnp.int32)
            for which, source in enumerate((segs, pars)):
                row = source[each : each + 1, rows - REACH :]
                numbers = jnp.where(at == 2 * which, row >> 7, numbers)
                numbers = jnp.where(at == 2 * which + 1, row & 127, numbers)
            numbers = numbers.astype(jnp.float32).astype(jnp.bfloat16)
            packed[each, 0, REACH:, :REACH] = numbers
            packed[each, 0, REACH:, REACH:] = jnp.zeros((INFO, keys.shape[2] - REACH), jnp.bfloat16)
            packed[each, 1, REACH:, :] = jnp.zeros((INFO, keys.shape[2]), jnp.bfloat16)
        for copy in pack_copies:
            copy.wait()
        pack_stores.append(start(packed.at[path], pack_outs[0]))
        pack_stores.append(start(packed.at[1 - path], pack_outs[1]))

    if pack and not last:
        store_pack()

    def column(row):
        return jnp.transpose(jnp.broadcast_to(row, (BLK, BLK)))

    def related(block, back):
        ours = pl.ds(pl.multiple_of(REACH + block * BLK, BLK), BLK)
        theirs = pl.ds(pl.multiple_of(REACH + (block - back) * BLK, BLK), BLK)
        key_seg = seg[:, theirs]
        query_seg, query_par = (column(seg[:, ours]), column(par[:, ours]))
        found = (key_seg == query_seg) | (key_seg == query_par) | (par[:, theirs] == key_seg)
        if back:
            return found & (first_block + block - back >= marks[block])
        lane = lax.broadcasted_iota(jnp.int32, (BLK, BLK), 1)
        return found & (lane <= lax.broadcasted_iota(jnp.int32, (BLK, BLK), 0))

    if corner:
        query_copy.wait()
        seen = related(first, 0).astype(jnp.float32).astype(jnp.bfloat16)
        turned = jnp.transpose(flipped(jnp.transpose(flipped(seen[:HALF]).astype(jnp.float32)).astype(jnp.bfloat16)).astype(jnp.float32))
        own_rows = pl.ds(pl.multiple_of(REACH + first * BLK, BLK), BLK)
        left, right = sides()
        low_bias = jnp.where(left & (seen[HALF:].astype(jnp.float32) > 0.5), 0.0, NEG)
        high_bias = jnp.where(right & (turned > 0.5), 0.0, NEG)
        between = jnp.logical_not(left | right)

        def ratios(query, key, mask):
            scores = product_t(query, key).reshape(group, HALF, BLK)
            own = jnp.sum(jnp.where(between[None], scores, 0.0), axis=-1, keepdims=True)
            scores = scores + mask[None]
            base = jnp.maximum(own, jnp.max(scores, axis=-1, keepdims=True) - RANGE / FACTOR)
            return jnp.exp2((scores - base) * FACTOR)

        for at in range(taken):
            key = kbuf[own_rows, at * HEAD : (at + 1) * HEAD]
            query = corner_q[:, at * width : (at + 1) * width]
            low = ratios(stacked(query[HALF:]), key, low_bias)
            high = ratios(stacked(flipped(query[:HALF])), flipped(key), high_bias)
            mixed = jnp.where(right[None], high, first.astype(jnp.float32))
            mixed = jnp.where(left[None], low, mixed).astype(jnp.bfloat16)
            value = vbuf[own_rows, at * HEAD : (at + 1) * HEAD]
            for g in range(group):
                place = slice(at * width + g * HEAD, at * width + (g + 1) * HEAD)
                corner_out[:HALF, place] = mixed[g]
                corner_out[HALF:, place] = value[g * 16 : (g + 1) * 16]
        corner_stores = []
        for at in range(taken):
            rows_to = pl.ds(len(items) * BLK + at * CORNER, CORNER)
            corner_stores.append(start(corner_out.at[:, pl.ds(at * width, width)], outs[0].at[rows_to]))

    def block_of(place):
        at = jnp.int32(items[-1])
        for other in range(len(items) - 1):
            at = jnp.where(place == other, jnp.int32(items[other]), at)
        return at + (first <= at).astype(jnp.int32)

    def build_bias(block):
        for back in range(TREE_MOST):
            at = (TREE_MOST - 1 - back) * BLK
            bias[:, at : at + BLK] = jnp.where(related(block, back), 0.0, NEG)

    def mixture(query, key, value):
        scores = product_t(stacked(query), key)
        scores = scores.reshape(group, BLK, SPAN) + bias[...][None]
        top = jnp.max(scores, axis=-1, keepdims=True)
        weights = jnp.exp2((scores - top) * FACTOR)
        totals = jnp.sum(weights, axis=-1, keepdims=True)
        rounded = weights.astype(jnp.bfloat16).reshape(group * BLK, SPAN)
        mixed = product(rounded, value)
        mixed = (mixed.reshape(group, BLK, HEAD) / totals).astype(jnp.bfloat16)
        return jnp.concatenate([mixed[g] for g in range(group)], axis=1)

    if last:
        rows_ready()
        build_bias(TREE_MOST)
        for copy in kv_copies:
            copy.wait()
        stores = []
        window = slice(TREE_MOST * BLK, TREE_MOST * BLK + SPAN)
        for at, copy in enumerate(query_copies):
            lanes = slice(at * HEAD, (at + 1) * HEAD)
            place = slice(at * width, (at + 1) * width)
            copy.wait()
            last_out[:, place] = mixture(last_q[:, place], kbuf[window, lanes], vbuf[window, lanes])
            stores.append(start(last_out.at[:, place], outs[0].at[:, place]))
            if pack and at == 0:
                store_pack()
        for copy in stores + pack_stores:
            copy.wait()
        return

    def body(skipped, taken, query_ref, out_ref):
        step = marks[count]
        marks[count] = step + 1
        block, head = (block_of(lax.div(step, taken)), lax.rem(step, taken))

        if not corner:
            pl.when(step == 0)(all_ready)

        pl.when(head == 0)(lambda: build_bias(block))
        window = pl.ds(pl.multiple_of(block * BLK, BLK), SPAN)
        at = pl.ds(pl.multiple_of((skipped + head) * HEAD, HEAD), HEAD)
        out_ref[...] = mixture(query_ref[0], kbuf[window, at], vbuf[window, at])

    for out, heads_here in zip(outs, groups):
        if not items:
            continue
        marks[count] = 0
        pltpu.emit_pipeline(
            functools.partial(body, heads_here[0] - heads[0], len(heads_here)),
            grid=(len(items), len(heads_here)),
            in_specs=[pl.BlockSpec((1, BLK, width), lambda i, h, at=heads_here[0]: (path, block_of(i), at + h))],
            out_specs=[pl.BlockSpec((BLK, width), lambda i, h: (i, h))],
        )(queries, out.at[pl.ds(0, len(items) * BLK)])
    if corner:
        for copy in corner_stores:
            copy.wait()
    for copy in pack_stores:
        copy.wait()


def attend(payload, groups, items, operands, after=(), halo=None, corner=False, pack=False, last=False, weight=0):
    lengths, queries, keys, values, seg, par = operands
    rows, columns = queries.shape[1:]
    width = columns // (keys.shape[2] // HEAD)
    count = rows // BLK
    heads = [head for group in groups for head in group]
    sizes = [(len(items) * BLK, len(group) * width) for group in groups]
    if corner:
        sizes[0] = (len(items) * BLK + len(heads) * CORNER, width)
    out_shape = [jax.ShapeDtypeStruct(size, jnp.bfloat16) for size in sizes]
    scratch = [
        pltpu.VMEM((REACH + rows, len(heads) * HEAD), jnp.bfloat16),
        pltpu.VMEM((REACH + rows, len(heads) * HEAD), jnp.bfloat16),
        pltpu.VMEM((BLK, SPAN), jnp.float32),
        pltpu.VMEM(seg.shape, jnp.int32),
        pltpu.VMEM(par.shape, jnp.int32),
        pltpu.VMEM((1, REACH + rows), jnp.int32),
        pltpu.VMEM((1, REACH + rows), jnp.int32),
        pltpu.SMEM(lengths.shape, jnp.int32),
        pltpu.SMEM((count + 1,), jnp.int32),
        pltpu.SemaphoreType.DMA((20,)),
    ]
    if halo is not None:
        scratch.append(pltpu.VMEM((INFO, keys.shape[2]), jnp.bfloat16))
    if corner:
        scratch.append(pltpu.VMEM((BLK, len(heads) * width), jnp.bfloat16))
        scratch.append(pltpu.VMEM((CORNER, len(heads) * width), jnp.bfloat16))
    if pack:
        packed = (2, 2, REACH + INFO, keys.shape[2])
        out_shape += [jax.ShapeDtypeStruct(packed[1:], jnp.bfloat16)] * 2
        scratch.append(pltpu.VMEM(packed, jnp.bfloat16))
    if last:
        scratch += [pltpu.VMEM((BLK, len(heads) * width), jnp.bfloat16)] * 2
    inputs = [lengths, queries, keys, values, seg, par] + ([] if halo is None else [halo])

    def kernel(*refs):
        refs = refs[: len(inputs)] + refs[len(inputs) + len(after) :]
        attend_kernel(payload, groups, items, corner, pack, halo is not None, last, *refs)

    return pl.pallas_call(
        kernel,
        out_shape=out_shape,
        in_specs=[HBM] * 6 + [ANY] * (len(inputs) - 6 + len(after)),
        out_specs=[ANY] * len(out_shape),
        scratch_shapes=scratch,
        compiler_params=pltpu.CompilerParams(vmem_limit_bytes=VMEM_LIMIT),
        cost_estimate=cost(weight),
    )(*inputs, *after)


def behind(value, *after):
    return pl.pallas_call(
        lambda *refs: None,
        out_shape=jax.ShapeDtypeStruct(value.shape, value.dtype),
        in_specs=[ANY] * (1 + len(after)),
        out_specs=ANY,
        input_output_aliases={0: 0},
        cost_estimate=cost(0),
    )(value, *after)


def place_kernel(pieces, aliased, *refs):
    refs = list(refs)
    sources = [[refs.pop(0)] if piece[1] else [refs.pop(0), refs.pop(0)] for piece in pieces]
    refs = refs[aliased:]
    forward, back = refs[:2]
    stages = refs[2 : 2 + len(pieces)]
    refs = refs[2 + len(pieces) :]
    blocks = {at: refs.pop(0) for at, piece in enumerate(pieces) if piece[0] == "corner"}
    in_sems, out_sems = refs
    width = forward.shape[1] // KV_HEADS
    group = width // HEAD
    where = lax.axis_index("pipe")
    even = lax.rem(where, 2) == 0
    edge = (where == 0) | (where == lax.axis_size("pipe") - 1)

    parts = []
    for at, (kind, _, _, items, top) in enumerate(pieces):
        if kind == "plain":
            parts += [(at, item * BLK, BLK, 0) for item in range(len(items))]
        else:
            parts.append((at, 0, stages[at].shape[0], top))

    def load(part, source):
        at, top, height, below = parts[part]
        view = (pl.ds(below + top, height), pl.ds(0, stages[at].shape[1]))
        return pltpu.make_async_copy(source.at[view], stages[at].at[pl.ds(top, height)], in_sems.at[part])

    for part, (at, _, _, _) in enumerate(parts):
        if len(sources[at]) == 1:
            load(part, sources[at][0]).start()
        else:
            pl.when(edge)(lambda: load(part, sources[at][1]).start())
            pl.when(jnp.logical_not(edge))(lambda: load(part, sources[at][0]).start())

    first = {}
    stores = []

    def store(at, source, block):
        _, swap, heads, _, _ = pieces[at]
        columns = pl.ds(heads[0] * width, len(heads) * width)
        rows = pl.ds(pl.multiple_of(block * BLK, BLK), BLK)
        for to_forward, target in ((even != swap, forward), (even == swap, back)):

            @pl.when(to_forward)
            def _():
                pltpu.make_async_copy(source, target.at[rows, columns], out_sems.at[len(stores)]).start()

        stores.append(pltpu.make_async_copy(source, forward.at[rows, columns], out_sems.at[len(stores)]))

    for part, (at, top, _, _) in enumerate(parts):
        kind, swap, heads, items, _ = pieces[at]
        load(part, sources[at][0]).wait()
        if kind == "plain":
            store(at, stages[at].at[pl.ds(top, BLK)], plain_block(first[swap], items[top // BLK]))
        elif swap not in first:
            tile = stages[at][:16, :HEAD].astype(jnp.float32)
            row = lax.broadcasted_iota(jnp.int32, tile.shape, 0)
            lane = lax.broadcasted_iota(jnp.int32, tile.shape, 1)
            first[swap] = jnp.sum(jnp.where((row == 0) & (lane == HALF), tile, 0.0)).astype(jnp.int32)

    left, right = sides()
    for at, decoded in blocks.items():
        value = stacked(stages[at][HALF:])
        turned = flipped(value)
        ratios = stacked(stages[at][:HALF].astype(jnp.float32)).reshape(group, HALF, BLK)

        def context(side, basis):
            kept = jnp.where(side[None], ratios, 0.0)
            totals = 1.0 + jnp.sum(kept, axis=-1, keepdims=True)
            mixed = product(kept.astype(jnp.bfloat16).reshape(group * HALF, BLK), basis)
            mixed = mixed.reshape(group, HALF, HEAD) + basis[HALF:].astype(jnp.float32)[None]
            mixed = (mixed / totals).astype(jnp.bfloat16)
            return jnp.concatenate([mixed[g] for g in range(group)], axis=1)

        decoded[HALF:] = context(left, value)
        decoded[:HALF] = flipped(context(right, turned))
        store(at, decoded, first[pieces[at][1]])
    for copy in stores:
        copy.wait()


def place(pieces, rows, outs=(), weight=0):
    arrays = [array for piece in pieces for array in piece[1]]
    columns = next(piece[1][0].shape[1] // len(piece[3]) for piece in pieces if piece[3]) * KV_HEADS
    shape = jax.ShapeDtypeStruct((rows, columns), jnp.bfloat16)
    width = columns // KV_HEADS
    corners = {"guide": (16, HEAD), "corner": (CORNER, width)}
    held = [corners.get(kind, (len(items) * BLK, len(heads) * width)) for kind, _, _, heads, items, _ in pieces]
    decoded = [(BLK, width) for piece in pieces if piece[0] == "corner"]
    return pl.pallas_call(
        functools.partial(place_kernel, [(piece[0],) + piece[2:] for piece in pieces], len(outs)),
        out_shape=[shape, shape],
        in_specs=[ANY] * len(arrays) + [HBM] * len(outs),
        out_specs=[HBM, HBM],
        scratch_shapes=[pltpu.VMEM(size, jnp.bfloat16) for size in held + decoded]
        + [pltpu.SemaphoreType.DMA((4 * len(pieces),))] * 2,
        input_output_aliases={len(arrays) + i: i for i in range(len(outs))},
        compiler_params=pltpu.CompilerParams(vmem_limit_bytes=24 * 1024 * 1024),
        cost_estimate=cost(weight),
    )(*arrays, *outs)


def cost(weight):
    return pl.CostEstimate(flops=1024 + weight * 1000000, bytes_accessed=1024, transcendentals=0)


PLACE_WEIGHT = 0
SWAP_WEIGHT = 2000
DIRECT_WEIGHT = 100000

SWAP = [(0, 1), (1, 0), (2, 3), (3, 2)]
DIAGONAL = [(1, 2), (2, 1)]
ACROSS = [(1, 3), (2, 0)]
ONWARD = [(3, 2), (0, 1)]


def on_device(queries, keys, values, segment, parent, tree_lengths):
    rows = queries.shape[2]
    operands = (tree_lengths[0], queries[0], keys[0], values[0], segment[0], parent[0])
    ring = [(source, source + 1) for source in range(lax.axis_size("dp") - 1)]
    every = tuple(range(KV_HEADS))

    (swap_0,) = attend(0, ((0,),), (2,), operands, last=True)
    got_0 = lax.ppermute(swap_0, "pipe", SWAP)
    swap_1, halo, far_halo = attend(0, ((1, 2, 3),), (2,), operands, after=(swap_0,), pack=True, last=True)
    got_1 = lax.ppermute(swap_1, "pipe", SWAP)
    halo = lax.ppermute(halo, "dp", ring)
    far_halo = lax.ppermute(far_halo, "dp", ring)
    (corner,) = attend(0, (every,), (), operands, after=(swap_1, got_0), corner=True)
    got_corner = lax.ppermute(corner, "pipe", SWAP)
    (swap_2,) = attend(0, (every,), (0, 1), operands, after=(corner,), halo=halo, weight=SWAP_WEIGHT)
    got_2 = lax.ppermute(swap_2, "pipe", SWAP)
    routed_1, routed_2 = attend(1, ((0,), (1,)), (0, 1, 2), operands, after=(swap_2,), halo=far_halo, corner=True)
    across_1 = lax.ppermute(routed_1, "pipe", ACROSS)
    direct_1, direct_2 = attend(
        1,
        ((2,), (3,)),
        (0, 1, 2),
        operands,
        after=(routed_1, got_1, got_corner),
        halo=far_halo,
        corner=True,
        weight=DIRECT_WEIGHT,
    )
    diagonal_1 = lax.ppermute(direct_1, "pipe", DIAGONAL)
    across_2 = lax.ppermute(behind(routed_2, direct_1), "pipe", ACROSS)
    diagonal_2 = lax.ppermute(behind(direct_2, across_2), "pipe", DIAGONAL)
    onward_1 = lax.ppermute(behind(across_1, direct_1), "pipe", ONWARD)
    onward_2 = lax.ppermute(behind(across_2, direct_1), "pipe", ONWARD)
    outs = place(
        [("corner", (got_corner,), True, (head,), (), head * CORNER) for head in every]
        + [
            ("plain", (got_0,), True, (0,), (2,), 0),
            ("plain", (got_1,), True, (1, 2, 3), (2,), 0),
            ("plain", (got_2,), True, every, (0, 1), 0),
        ],
        rows,
        weight=PLACE_WEIGHT,
    )
    below = TREE_MOST * BLK
    onward_1, diagonal_1 = ((onward_1, routed_1), (diagonal_1, direct_1))
    outs = place(
        [
            ("corner", onward_1, False, (0,), (), below),
            ("corner", onward_1, False, (1,), (), below + CORNER),
            ("corner", diagonal_1, False, (2,), (), below),
            ("corner", diagonal_1, False, (3,), (), below + CORNER),
            ("plain", onward_1, False, (0,), (0, 1, 2), 0),
            ("plain", diagonal_1, False, (2,), (0, 1, 2), 0),
        ],
        rows,
        outs,
    )
    forward, back = place(
        [
            ("guide", diagonal_1, False, (), (), below),
            ("plain", (onward_2, routed_2), False, (1,), (0, 1, 2), 0),
            ("plain", (diagonal_2, direct_2), False, (3,), (0, 1, 2), 0),
        ],
        rows,
        outs,
    )
    return (forward[None], back[None])


def solution(mesh):
    return jax.shard_map(
        on_device,
        mesh=mesh,
        in_specs=(
            P("pipe", None, "dp", None),
            P("pipe", None, "dp", None),
            P("pipe", None, "dp", None),
            P("pipe", None, "dp"),
            P("pipe", None, "dp"),
            P("pipe", None, None),
        ),
        out_specs=(P("pipe", "dp", None), P("pipe", "dp", None)),
        check_vma=False,
    )
```

```python
import functools
import math

import jax
import jax.numpy as jnp
from jax import lax
from jax.experimental import pallas as pl
from jax.experimental.pallas import tpu as pltpu
from jax.sharding import PartitionSpec as P

BLK = 128
TREE_MOST = 3
KV_HEADS = 4
HEAD = 128
REACH = (TREE_MOST - 1) * BLK
SPAN = TREE_MOST * BLK
NEG = -1e30
FACTOR = math.log2(math.e) / math.sqrt(HEAD)

HALF = BLK // 2
CORNER = HALF + 16
INFO = 16
RANGE = 80.0
VMEM_LIMIT = 60 * 1024 * 1024

ANY = pl.BlockSpec(memory_space=pl.ANY)
HBM = pl.BlockSpec(memory_space=pltpu.HBM)
VMEM = pl.BlockSpec(memory_space=pltpu.VMEM)


def flipped(array):
    count = array.shape[0]
    rows = lax.broadcasted_iota(jnp.int32, (count, count), 0)
    lanes = lax.broadcasted_iota(jnp.int32, (count, count), 1)
    swap = (rows + lanes == count - 1).astype(jnp.bfloat16)
    return jnp.dot(swap, array, preferred_element_type=jnp.float32).astype(jnp.bfloat16)


def stacked(array):
    return jnp.concatenate([array[:, at : at + HEAD] for at in range(0, array.shape[1], HEAD)], axis=0)


def product(left, right):
    return jnp.dot(left, right, preferred_element_type=jnp.float32)


def product_t(left, right):
    return lax.dot_general(left, right, (((1,), (1,)), ((), ())), preferred_element_type=jnp.float32)


def sides():
    lane = lax.broadcasted_iota(jnp.int32, (HALF, BLK), 1)
    gap = lax.broadcasted_iota(jnp.int32, (HALF, BLK), 0) + HALF
    return (lane < gap, lane > gap)


def plain_block(first, at):
    return at + (first <= at).astype(jnp.int32)


def attend_kernel(payload, groups, items, corner, pack, halo, last, resident, *refs):
    heads = [head for group in groups for head in group]
    refs = list(refs)
    lengths_in, queries, keys, values, seg_in, par_in = refs[:6]
    refs = refs[6:]
    halo_in = refs.pop(0) if halo else None
    outs = [refs.pop(0) for _ in groups]
    if resident:
        refs.pop(0)
    pack_outs = [refs.pop(0), refs.pop(0)] if pack else None
    kbuf, vbuf, bias, segs, pars, seg, par, lengths, marks, sems = refs[:10]
    refs = refs[10:]
    if halo:
        info = refs.pop(0)
    if corner:
        corner_q, corner_out = refs[:2]
        refs = refs[2:]
    if pack:
        packed = refs.pop(0)
    if last:
        last_q, last_out = refs[:2]
    rows = keys.shape[1]
    kv_heads = keys.shape[2] // HEAD
    width = queries.shape[2] // kv_heads
    group = width // HEAD
    count = rows // BLK
    taken = len(heads)
    path = lax.rem(lax.axis_index("pipe"), 2)
    path = path if payload == 0 else 1 - path
    first_block = lax.axis_index("dp") * count
    lanes = pl.ds(heads[0] * HEAD, taken * HEAD)

    started = []

    def start(source, target):
        copy = pltpu.make_async_copy(source, target, sems.at[len(started)])
        copy.start()
        started.append(copy)
        return copy

    lengths_copy = start(lengths_in, lengths)
    row_copies = [start(seg_in, segs), start(par_in, pars)]
    query_copies = []
    if last:
        for at, head in enumerate(heads):
            source = queries.at[path, pl.ds(TREE_MOST * BLK, BLK), pl.ds(head * width, width)]
            query_copies.append(start(source, last_q.at[:, pl.ds(at * width, width)]))
    kv_copies = []
    for which, (source, target) in enumerate(((keys, kbuf), (values, vbuf))):
        kv_copies.append(start(source.at[path, :, lanes], target.at[pl.ds(REACH, rows)]))
        if halo:
            kv_copies.append(start(halo_in.at[which, pl.ds(0, REACH), lanes], target.at[pl.ds(0, REACH)]))
    if halo:
        row_copies.append(start(halo_in.at[0, pl.ds(REACH, INFO)], info))
    pack_copies = []
    if pack:
        for each in range(2):
            for which, source in enumerate((keys, values)):
                source = source.at[each, pl.ds(rows - REACH, REACH)]
                pack_copies.append(start(source, packed.at[each, which, pl.ds(0, REACH)]))

    lengths_copy.wait()

    def step(entry, carry):
        end, begins = carry
        end = end + lengths[path, entry]
        return (end, tuple(jnp.where(end <= first_block + at, end, begin) for at, begin in enumerate(begins)))

    zero = jnp.int32(0)
    _, begins = lax.fori_loop(0, lengths.shape[1], step, (zero, (zero,) * count), unroll=8)
    first = jnp.int32(TREE_MOST - 1)
    for at in reversed(range(count)):
        marks[at] = begins[at]
        if at < TREE_MOST - 1:
            first = jnp.where(begins[at] == first_block + at, at, first)
    if corner:
        columns = pl.ds(heads[0] * width, taken * width)
        query_copy = start(queries.at[path, pl.ds(pl.multiple_of(first * BLK, BLK), BLK), columns], corner_q)

    def rows_ready():
        for copy in row_copies:
            copy.wait()
        for source, target in ((segs, seg), (pars, par)):
            target[:, REACH:] = jnp.where(path == 0, source[0:1], source[1:2])
        if halo:
            numbers = info[...].astype(jnp.float32)
            seg[:, :REACH] = (numbers[0:1, :REACH] * 128.0 + numbers[1:2, :REACH]).astype(jnp.int32)
            par[:, :REACH] = (numbers[2:3, :REACH] * 128.0 + numbers[3:4, :REACH]).astype(jnp.int32)

    def all_ready():
        rows_ready()
        for copy in kv_copies:
            copy.wait()

    if corner:
        all_ready()
    pack_stores = []

    def store_pack():
        for each in range(2):
            at = lax.broadcasted_iota(jnp.int32, (INFO, REACH), 0)
            numbers = jnp.zeros((INFO, REACH), jnp.int32)
            for which, source in enumerate((segs, pars)):
                row = source[each : each + 1, rows - REACH :]
                numbers = jnp.where(at == 2 * which, row >> 7, numbers)
                numbers = jnp.where(at == 2 * which + 1, row & 127, numbers)
            numbers = numbers.astype(jnp.float32).astype(jnp.bfloat16)
            packed[each, 0, REACH:, :REACH] = numbers
            packed[each, 0, REACH:, REACH:] = jnp.zeros((INFO, keys.shape[2] - REACH), jnp.bfloat16)
            packed[each, 1, REACH:, :] = jnp.zeros((INFO, keys.shape[2]), jnp.bfloat16)
        for copy in pack_copies:
            copy.wait()
        pack_stores.append(start(packed.at[path], pack_outs[0]))
        pack_stores.append(start(packed.at[1 - path], pack_outs[1]))

    if pack and not last:
        store_pack()

    def column(row):
        return jnp.transpose(jnp.broadcast_to(row, (BLK, BLK)))

    def related(block, back):
        ours = pl.ds(pl.multiple_of(REACH + block * BLK, BLK), BLK)
        theirs = pl.ds(pl.multiple_of(REACH + (block - back) * BLK, BLK), BLK)
        key_seg = seg[:, theirs]
        query_seg, query_par = (column(seg[:, ours]), column(par[:, ours]))
        found = (key_seg == query_seg) | (key_seg == query_par) | (par[:, theirs] == key_seg)
        if back:
            return found & (first_block + block - back >= marks[block])
        lane = lax.broadcasted_iota(jnp.int32, (BLK, BLK), 1)
        return found & (lane <= lax.broadcasted_iota(jnp.int32, (BLK, BLK), 0))

    if corner:
        query_copy.wait()
        seen = related(first, 0).astype(jnp.float32).astype(jnp.bfloat16)
        turned = jnp.transpose(flipped(jnp.transpose(flipped(seen[:HALF]).astype(jnp.float32)).astype(jnp.bfloat16)).astype(jnp.float32))
        own_rows = pl.ds(pl.multiple_of(REACH + first * BLK, BLK), BLK)
        left, right = sides()
        low_bias = jnp.where(left & (seen[HALF:].astype(jnp.float32) > 0.5), 0.0, NEG)
        high_bias = jnp.where(right & (turned > 0.5), 0.0, NEG)
        between = jnp.logical_not(left | right)

        def ratios(query, key, mask):
            scores = product_t(query, key).reshape(group, HALF, BLK)
            own = jnp.sum(jnp.where(between[None], scores, 0.0), axis=-1, keepdims=True)
            scores = scores + mask[None]
            base = jnp.maximum(own, jnp.max(scores, axis=-1, keepdims=True) - RANGE / FACTOR)
            return jnp.exp2((scores - base) * FACTOR)

        for at in range(taken):
            key = kbuf[own_rows, at * HEAD : (at + 1) * HEAD]
            query = corner_q[:, at * width : (at + 1) * width]
            low = ratios(stacked(query[HALF:]), key, low_bias)
            high = ratios(stacked(flipped(query[:HALF])), flipped(key), high_bias)
            mixed = jnp.where(right[None], high, first.astype(jnp.float32))
            mixed = jnp.where(left[None], low, mixed).astype(jnp.bfloat16)
            value = vbuf[own_rows, at * HEAD : (at + 1) * HEAD]
            for g in range(group):
                place = slice(at * width + g * HEAD, at * width + (g + 1) * HEAD)
                corner_out[:HALF, place] = mixed[g]
                corner_out[HALF:, place] = value[g * 16 : (g + 1) * 16]
        corner_stores = []
        for at in range(taken):
            rows_to = pl.ds(len(items) * BLK + at * CORNER, CORNER)
            corner_stores.append(start(corner_out.at[:, pl.ds(at * width, width)], outs[0].at[rows_to]))

    def block_of(place):
        at = jnp.int32(items[-1])
        for other in range(len(items) - 1):
            at = jnp.where(place == other, jnp.int32(items[other]), at)
        return at + (first <= at).astype(jnp.int32)

    def build_bias(block):
        for back in range(TREE_MOST):
            at = (TREE_MOST - 1 - back) * BLK
            bias[:, at : at + BLK] = jnp.where(related(block, back), 0.0, NEG)

    def mixture(query, key, value):
        scores = product_t(stacked(query), key)
        scores = scores.reshape(group, BLK, SPAN) + bias[...][None]
        top = jnp.max(scores, axis=-1, keepdims=True)
        weights = jnp.exp2((scores - top) * FACTOR)
        totals = jnp.sum(weights, axis=-1, keepdims=True)
        rounded = weights.astype(jnp.bfloat16).reshape(group * BLK, SPAN)
        mixed = product(rounded, value)
        mixed = (mixed.reshape(group, BLK, HEAD) / totals).astype(jnp.bfloat16)
        return jnp.concatenate([mixed[g] for g in range(group)], axis=1)

    if last:
        rows_ready()
        build_bias(TREE_MOST)
        for copy in kv_copies:
            copy.wait()
        stores = []
        window = slice(TREE_MOST * BLK, TREE_MOST * BLK + SPAN)
        for at, copy in enumerate(query_copies):
            lanes = slice(at * HEAD, (at + 1) * HEAD)
            place = slice(at * width, (at + 1) * width)
            copy.wait()
            if resident:
                outs[0][:, place] = mixture(last_q[:, place], kbuf[window, lanes], vbuf[window, lanes])
            else:
                last_out[:, place] = mixture(last_q[:, place], kbuf[window, lanes], vbuf[window, lanes])
                stores.append(start(last_out.at[:, place], outs[0].at[:, place]))
            if pack and at == 0:
                store_pack()
        for copy in stores + pack_stores:
            copy.wait()
        return

    def body(skipped, taken, query_ref, out_ref):
        step = marks[count]
        marks[count] = step + 1
        block, head = (block_of(lax.div(step, taken)), lax.rem(step, taken))

        if not corner:
            pl.when(step == 0)(all_ready)

        pl.when(head == 0)(lambda: build_bias(block))
        window = pl.ds(pl.multiple_of(block * BLK, BLK), SPAN)
        at = pl.ds(pl.multiple_of((skipped + head) * HEAD, HEAD), HEAD)
        out_ref[...] = mixture(query_ref[0], kbuf[window, at], vbuf[window, at])

    for out, heads_here in zip(outs, groups):
        if not items:
            continue
        marks[count] = 0
        pltpu.emit_pipeline(
            functools.partial(body, heads_here[0] - heads[0], len(heads_here)),
            grid=(len(items), len(heads_here)),
            in_specs=[pl.BlockSpec((1, BLK, width), lambda i, h, at=heads_here[0]: (path, block_of(i), at + h))],
            out_specs=[pl.BlockSpec((BLK, width), lambda i, h: (i, h))],
        )(queries, out.at[pl.ds(0, len(items) * BLK)])
    if corner:
        for copy in corner_stores:
            copy.wait()
    for copy in pack_stores:
        copy.wait()


def attend(payload, groups, items, operands, after=(), halo=None, corner=False, pack=False, last=False, resident=False, weight=0):
    lengths, queries, keys, values, seg, par = operands
    rows, columns = queries.shape[1:]
    width = columns // (keys.shape[2] // HEAD)
    count = rows // BLK
    heads = [head for group in groups for head in group]
    sizes = [(len(items) * BLK, len(group) * width) for group in groups]
    if corner:
        sizes[0] = (len(items) * BLK + len(heads) * CORNER, width)
    out_shape = [jax.ShapeDtypeStruct(size, jnp.bfloat16) for size in sizes]
    scratch = [
        pltpu.VMEM((REACH + rows, len(heads) * HEAD), jnp.bfloat16),
        pltpu.VMEM((REACH + rows, len(heads) * HEAD), jnp.bfloat16),
        pltpu.VMEM((BLK, SPAN), jnp.float32),
        pltpu.VMEM(seg.shape, jnp.int32),
        pltpu.VMEM(par.shape, jnp.int32),
        pltpu.VMEM((1, REACH + rows), jnp.int32),
        pltpu.VMEM((1, REACH + rows), jnp.int32),
        pltpu.SMEM(lengths.shape, jnp.int32),
        pltpu.SMEM((count + 1,), jnp.int32),
        pltpu.SemaphoreType.DMA((20,)),
    ]
    if halo is not None:
        scratch.append(pltpu.VMEM((INFO, keys.shape[2]), jnp.bfloat16))
    if corner:
        scratch.append(pltpu.VMEM((BLK, len(heads) * width), jnp.bfloat16))
        scratch.append(pltpu.VMEM((CORNER, len(heads) * width), jnp.bfloat16))
    if pack:
        packed = (2, 2, REACH + INFO, keys.shape[2])
        out_shape += [jax.ShapeDtypeStruct(packed[1:], jnp.bfloat16)] * 2
        scratch.append(pltpu.VMEM(packed, jnp.bfloat16))
    if last:
        scratch += [pltpu.VMEM((BLK, len(heads) * width), jnp.bfloat16)] * 2
    if resident:
        out_shape = [pltpu.VMEM(sizes[0], jnp.bfloat16), jax.ShapeDtypeStruct((8, HEAD), jnp.float32)]
    inputs = [lengths, queries, keys, values, seg, par] + ([] if halo is None else [halo])

    def kernel(*refs):
        refs = refs[: len(inputs)] + refs[len(inputs) + len(after) :]
        attend_kernel(payload, groups, items, corner, pack, halo is not None, last, resident, *refs)

    return pl.pallas_call(
        kernel,
        out_shape=out_shape,
        in_specs=[HBM] * 6 + [ANY] * (len(inputs) - 6 + len(after)),
        out_specs=[VMEM, ANY] if resident else [ANY] * len(out_shape),
        scratch_shapes=scratch,
        compiler_params=pltpu.CompilerParams(vmem_limit_bytes=VMEM_LIMIT),
        cost_estimate=cost(weight),
    )(*inputs, *after)


def behind(value, *after):
    return pl.pallas_call(
        lambda *refs: None,
        out_shape=jax.ShapeDtypeStruct(value.shape, value.dtype),
        in_specs=[ANY] * (1 + len(after)),
        out_specs=ANY,
        input_output_aliases={0: 0},
        cost_estimate=cost(0),
    )(value, *after)


def place_kernel(pieces, aliased, resident, *refs):
    refs = list(refs)
    sources = [[refs.pop(0)] if piece[1] else [refs.pop(0), refs.pop(0)] for piece in pieces]
    refs = refs[aliased:]
    forward, back = refs[:2]
    stages = refs[2 : 2 + len(pieces)]
    refs = refs[2 + len(pieces) :]
    blocks = {at: refs.pop(0) for at, piece in enumerate(pieces) if piece[0] == "corner"}
    in_sems, out_sems = refs
    width = forward.shape[1] // KV_HEADS
    group = width // HEAD
    where = lax.axis_index("pipe")
    even = lax.rem(where, 2) == 0
    edge = (where == 0) | (where == lax.axis_size("pipe") - 1)

    parts = []
    for at, (kind, _, _, items, top) in enumerate(pieces):
        if kind == "plain" and resident:
            parts.append((at, 0, 0, 0))
        elif kind == "plain":
            parts += [(at, item * BLK, BLK, 0) for item in range(len(items))]
        else:
            parts.append((at, 0, stages[at].shape[0], top))

    def load(part, source):
        at, top, height, below = parts[part]
        view = (pl.ds(below + top, height), pl.ds(0, stages[at].shape[1]))
        return pltpu.make_async_copy(source.at[view], stages[at].at[pl.ds(top, height)], in_sems.at[part])

    for part, (at, _, height, _) in enumerate(parts):
        if height == 0:
            continue
        if len(sources[at]) == 1:
            load(part, sources[at][0]).start()
        else:
            pl.when(edge)(lambda: load(part, sources[at][1]).start())
            pl.when(jnp.logical_not(edge))(lambda: load(part, sources[at][0]).start())

    first = {}
    stores = []

    def store(at, source, block, where_from=None):
        _, swap, heads, _, _ = pieces[at]
        columns = pl.ds(heads[0] * width, len(heads) * width)
        rows = pl.ds(pl.multiple_of(block * BLK, BLK), BLK)
        for to_forward, target in ((even != swap, forward), (even == swap, back)):

            @pl.when(to_forward if where_from is None else to_forward & where_from)
            def _():
                pltpu.make_async_copy(source, target.at[rows, columns], out_sems.at[len(stores)]).start()

        stores.append(pltpu.make_async_copy(source, forward.at[rows, columns], out_sems.at[len(stores)]))

    for part, (at, top, height, _) in enumerate(parts):
        kind, swap, heads, items, _ = pieces[at]
        if height == 0:
            for index, item in enumerate(items):
                view = pl.ds(index * BLK, BLK)
                store(at, sources[at][1].at[view], plain_block(first[swap], item), edge)
                stores.pop()
                store(at, sources[at][0].at[view], plain_block(first[swap], item), jnp.logical_not(edge))
            continue
        load(part, sources[at][0]).wait()
        if kind == "plain":
            store(at, stages[at].at[pl.ds(top, BLK)], plain_block(first[swap], items[top // BLK]))
        elif swap not in first:
            tile = stages[at][:16, :HEAD].astype(jnp.float32)
            row = lax.broadcasted_iota(jnp.int32, tile.shape, 0)
            lane = lax.broadcasted_iota(jnp.int32, tile.shape, 1)
            first[swap] = jnp.sum(jnp.where((row == 0) & (lane == HALF), tile, 0.0)).astype(jnp.int32)

    left, right = sides()
    for at, decoded in blocks.items():
        value = stacked(stages[at][HALF:])
        turned = flipped(value)
        ratios = stacked(stages[at][:HALF].astype(jnp.float32)).reshape(group, HALF, BLK)

        def context(side, basis):
            kept = jnp.where(side[None], ratios, 0.0)
            totals = 1.0 + jnp.sum(kept, axis=-1, keepdims=True)
            mixed = product(kept.astype(jnp.bfloat16).reshape(group * HALF, BLK), basis)
            mixed = mixed.reshape(group, HALF, HEAD) + basis[HALF:].astype(jnp.float32)[None]
            mixed = (mixed / totals).astype(jnp.bfloat16)
            return jnp.concatenate([mixed[g] for g in range(group)], axis=1)

        decoded[HALF:] = context(left, value)
        decoded[:HALF] = flipped(context(right, turned))
        store(at, decoded, first[pieces[at][1]])
    for copy in stores:
        copy.wait()


def place(pieces, rows, outs=(), resident=False):
    arrays = [array for piece in pieces for array in piece[1]]
    columns = next(piece[1][0].shape[1] // len(piece[3]) for piece in pieces if piece[3]) * KV_HEADS
    shape = jax.ShapeDtypeStruct((rows, columns), jnp.bfloat16)
    width = columns // KV_HEADS
    corners = {"guide": (16, HEAD), "corner": (CORNER, width)}
    held = [corners.get(kind, (len(items) * BLK, len(heads) * width)) for kind, _, _, heads, items, _ in pieces]
    specs = [ANY] * len(arrays)
    if resident:
        held = [corners.get(piece[0], (16, HEAD)) for piece in pieces]
        specs = [VMEM if piece[0] == "plain" else ANY for piece in pieces for _ in piece[1]]
        arrays = [
            pltpu.with_memory_space_constraint(array, pltpu.VMEM) if spec is VMEM else array
            for array, spec in zip(arrays, specs)
        ]
    decoded = [(BLK, width) for piece in pieces if piece[0] == "corner"]
    return pl.pallas_call(
        functools.partial(place_kernel, [(piece[0],) + piece[2:] for piece in pieces], len(outs), resident),
        out_shape=[shape, shape],
        in_specs=specs + [HBM] * len(outs),
        out_specs=[HBM, HBM],
        scratch_shapes=[pltpu.VMEM(size, jnp.bfloat16) for size in held + decoded]
        + [pltpu.SemaphoreType.DMA((4 * len(pieces),))] * 2,
        input_output_aliases={len(arrays) + i: i for i in range(len(outs))},
        compiler_params=pltpu.CompilerParams(vmem_limit_bytes=24 * 1024 * 1024),
        cost_estimate=cost(0),
    )(*arrays, *outs)


def cost(weight):
    return pl.CostEstimate(flops=1024 + weight * 1000000, bytes_accessed=1024, transcendentals=0)


SWAP_WEIGHT = 2000
DIRECT_WEIGHT = 100000

SWAP = [(0, 1), (1, 0), (2, 3), (3, 2)]
DIAGONAL = [(1, 2), (2, 1)]
ACROSS = [(1, 3), (2, 0)]
ONWARD = [(3, 2), (0, 1)]


def on_device(queries, keys, values, segment, parent, tree_lengths):
    rows = queries.shape[2]
    operands = (tree_lengths[0], queries[0], keys[0], values[0], segment[0], parent[0])
    ring = [(source, source + 1) for source in range(lax.axis_size("dp") - 1)]
    every = tuple(range(KV_HEADS))

    swap_0, made_0 = attend(0, ((0,),), (2,), operands, last=True, resident=True)
    got_0 = lax.ppermute(swap_0, "pipe", SWAP)
    swap_1, halo, far_halo = attend(0, ((1, 2, 3),), (2,), operands, after=(made_0,), pack=True, last=True)
    got_1 = lax.ppermute(swap_1, "pipe", SWAP)
    halo = lax.ppermute(halo, "dp", ring)
    far_halo = lax.ppermute(far_halo, "dp", ring)
    (corner,) = attend(0, (every,), (), operands, after=(swap_1, got_0), corner=True)
    got_corner = lax.ppermute(corner, "pipe", SWAP)
    (swap_2,) = attend(0, (every,), (0, 1), operands, after=(corner,), halo=halo, weight=SWAP_WEIGHT)
    got_2 = lax.ppermute(swap_2, "pipe", SWAP)
    routed_1, routed_2 = attend(1, ((0,), (1,)), (0, 1, 2), operands, after=(swap_2,), halo=far_halo, corner=True)
    across_1 = lax.ppermute(routed_1, "pipe", ACROSS)
    direct_1, direct_2 = attend(
        1,
        ((2,), (3,)),
        (0, 1, 2),
        operands,
        after=(routed_1, got_1, got_corner),
        halo=far_halo,
        corner=True,
        weight=DIRECT_WEIGHT,
    )
    diagonal_1 = lax.ppermute(direct_1, "pipe", DIAGONAL)
    across_2 = lax.ppermute(behind(routed_2, direct_1), "pipe", ACROSS)
    diagonal_2 = lax.ppermute(behind(direct_2, across_2), "pipe", DIAGONAL)
    onward_1 = lax.ppermute(behind(across_1, direct_1), "pipe", ONWARD)
    onward_2 = lax.ppermute(behind(across_2, direct_1), "pipe", ONWARD)
    outs = place(
        [("corner", (got_corner,), True, (head,), (), head * CORNER) for head in every]
        + [
            ("plain", (got_0,), True, (0,), (2,), 0),
            ("plain", (got_1,), True, (1, 2, 3), (2,), 0),
            ("plain", (got_2,), True, every, (0, 1), 0),
        ],
        rows,
    )
    below = TREE_MOST * BLK
    onward_1, diagonal_1 = ((onward_1, routed_1), (diagonal_1, direct_1))
    outs = place(
        [
            ("corner", onward_1, False, (0,), (), below),
            ("corner", onward_1, False, (1,), (), below + CORNER),
            ("corner", diagonal_1, False, (2,), (), below),
            ("corner", diagonal_1, False, (3,), (), below + CORNER),
            ("plain", onward_1, False, (0,), (0, 1, 2), 0),
            ("plain", diagonal_1, False, (2,), (0, 1, 2), 0),
        ],
        rows,
        outs,
    )
    forward, back = place(
        [
            ("guide", diagonal_1, False, (), (), below),
            ("plain", (onward_2, routed_2), False, (1,), (0, 1, 2), 0),
            ("plain", (diagonal_2, direct_2), False, (3,), (0, 1, 2), 0),
        ],
        rows,
        outs,
        resident=True,
    )
    return (forward[None], back[None])


def solution(mesh):
    return jax.shard_map(
        on_device,
        mesh=mesh,
        in_specs=(
            P("pipe", None, "dp", None),
            P("pipe", None, "dp", None),
            P("pipe", None, "dp", None),
            P("pipe", None, "dp"),
            P("pipe", None, "dp"),
            P("pipe", None, None),
        ),
        out_specs=(P("pipe", "dp", None), P("pipe", "dp", None)),
        check_vma=False,
    )
```
